512 devices in a mesh: section: 8 (over x, core), dp: 64 (over y, z).
Axes of the slice: x: 4, y: 8, z: 8, core: 2. Of those that a mesh axis runs over, the one named last changes fastest.
Arguments:
- gradients: bfloat16 [8, 64, 192, 3072], P('section', 'dp'), may hold values from -800 to 800
- error_buffers: bfloat16 [8, 64, 192, 3072], P('section', 'dp'), may hold values from -6 to 6
- initial_q: float32 [8, 192, 32], P('section'), may hold values from -6 to 6
- master: float32 [8, 192, 3072], P('section', None, 'dp'), may hold values from -0.75 to 0.75
- first_moment: float32 [8, 192, 3072], P('section', None, 'dp'), may hold values from -0.046875 to 0.046875
- second_moment: float32 [8, 192, 3072], P('section', None, 'dp'), may hold values from 1e-07 to 1e-05
Outputs:
- new_errors: bfloat16 [8, 64, 192, 3072], P('section', 'dp')
- q_factor: float32 [8, 192, 32], P('section')
- new_master: float32 [8, 192, 3072], P('section', None, 'dp')
- new_first: float32 [8, 192, 3072], P('section', None, 'dp')
- new_second: float32 [8, 192, 3072], P('section', None, 'dp')
- gathered_weights: bfloat16 [8, 192, 3072], P('section')
The draws below stay inside these ranges and needn't reach their ends.
All inputs are finite; a program needn't handle non-finite values.
Results may differ from the reference program's by a relative error of at most 0.00045.
Values may be sent and summed in bfloat16 or wider, within the bound.
A program may use at most 64 MiB of HBM per device.

```python
import math
import jax
import jax.numpy as jnp
from jax import lax

COLS = 3072
SLAB = 192
RANK = 32
STEP = 10
SECTIONS = 8
REPLICAS = 64


def draw_gradients(key, part):
    key = jax.random.fold_in(key, 17)
    subkeys = jax.random.split(key, 3)
    full_shape = (SECTIONS, REPLICAS, SLAB, COLS)
    row_scale = 10.0 ** (0.5 * jax.random.uniform(subkeys[0], (SECTIONS, 1, SLAB, 1), jnp.float32))
    col_scale = 10.0 ** (0.5 * jax.random.uniform(subkeys[1], (SECTIONS, 1, 1, COLS), jnp.float32))
    replica_pos = jnp.arange(REPLICAS, dtype=jnp.float32).reshape(1, REPLICAS, 1, 1) / max(REPLICAS - 1, 1)
    section_pos = jnp.arange(SECTIONS, dtype=jnp.float32).reshape(SECTIONS, 1, 1, 1) / max(SECTIONS - 1, 1)
    base_draw = jax.random.truncated_normal(subkeys[2], -4.0, 4.0, full_shape, jnp.float32)
    rise_factor = 2.0
    values = base_draw * row_scale * col_scale * (1.0 + rise_factor * replica_pos) * (1.0 + 2.0 * section_pos)
    return values.astype(jnp.bfloat16)


def steps_of(rng, extent, cuts, low, top_value):
    loudness, own = 1.0, jax.random.fold_in(rng, 6)
    for dim, blocks in cuts:
        draws = jnp.exp(jax.random.uniform(jax.random.fold_in(own, dim), (blocks,), jnp.float32, low / len(cuts), top_value / len(cuts)))
        loudness = loudness * jnp.repeat(draws, extent[dim] // blocks).reshape([-1 if axis == dim else 1 for axis in range(len(extent))])
    return loudness


def bell_draw(rng, dims, deviation, limit, shards=(), kind=jnp.bfloat16):
    entries = jax.random.normal(rng, dims, jnp.float32) * deviation
    if len(shards) > 0:
        entries = steps_of(rng, dims, shards, -0.22, 0.18) * entries
    return jnp.clip(entries, min=-limit, max=limit).astype(kind)


def setup_inputs(seed: int = 0) -> dict:
    key_of = jax.random.split(jax.random.key(seed), 7)
    gradients = draw_gradients(jax.random.fold_in(key_of[6], 71), 0)
    error_buffers = bell_draw(key_of[1], (SECTIONS, REPLICAS, SLAB, COLS), 1.0, 6.0, ((0, 8), (1, 64)))
    initial_q = bell_draw(key_of[2], (SECTIONS, SLAB, RANK), 1.0, 6.0, ((0, 8),), jnp.float32)
    master = bell_draw(key_of[3], (SECTIONS, SLAB, COLS), 0.05, 0.75, ((0, 8), (2, 64)), jnp.float32)
    first_moment = bell_draw(key_of[4], (SECTIONS, SLAB, COLS), 0.003, 0.046875, ((0, 8), (2, 64)), jnp.float32)
    second_moment = jnp.clip(jnp.exp(math.log(9.999999747378752e-06) - 4.6051701 * jax.random.uniform(key_of[5], (SECTIONS, SLAB, COLS), jnp.float32) ** steps_of(key_of[5], (SECTIONS, SLAB, COLS), ((0, 8), (2, 64)), -0.2, 0.2)), 1.0000000116860974e-07, 9.999999747378752e-06)
    return {"gradients": gradients, "error_buffers": error_buffers, "initial_q": initial_q, "master": master, "first_moment": first_moment, "second_moment": second_moment}


beta_one = 0.9
beta_two = 0.999
adam_epsilon = 1e-08
learn_rate = 0.02
clip_limit = 16.0

def orthonormal(projected):
    gram_matrix = jnp.dot(projected.T, projected, precision=lax.Precision.HIGHEST)
    cholesky_factor = jnp.linalg.cholesky(gram_matrix)
    solved = jax.scipy.linalg.solve_triangular(cholesky_factor, projected.T, lower=True)
    return solved.T

def one_section(inputs):
    grad_section, error_section, q_section = inputs
    combined = grad_section.astype(jnp.float32) + error_section.astype(jnp.float32)
    projected = jnp.einsum('iac,ar->cr', combined, q_section, precision=lax.Precision.HIGHEST)
    ortho_basis = orthonormal(projected)
    right_factor = jnp.einsum('iac,cr->ar', combined, ortho_basis, precision=lax.Precision.HIGHEST) / REPLICAS
    approx = jnp.dot(right_factor, ortho_basis.T, precision=lax.Precision.HIGHEST)
    errors_out = (combined - approx[None]).astype(jnp.bfloat16)
    return (errors_out, right_factor, approx)

def reference(gradients, error_buffers, initial_q, master, first_moment, second_moment):
    new_errors, q_factor, approx = lax.map(one_section, (gradients, error_buffers, initial_q))
    squares = jnp.sum(approx * approx)
    clip_factor = jnp.minimum(1.0, clip_limit / jnp.sqrt(squares))
    scaled = clip_factor * approx
    new_first = beta_one * first_moment + (1.0 - beta_one) * scaled
    new_second = beta_two * second_moment + (1.0 - beta_two) * scaled * scaled
    adam_step = new_first / (1.0 - beta_one ** STEP) / (jnp.sqrt(new_second / (1.0 - beta_two ** STEP)) + adam_epsilon)
    new_master = master - learn_rate * adam_step
    gathered_weights = new_master.astype(jnp.bfloat16)
    return (new_errors, q_factor, new_master, new_first, new_second, gathered_weights)
```

```python
import functools

import jax
import jax.numpy as jnp
from jax import lax
from jax.experimental import pallas as pl
from jax.experimental.pallas import tpu as pltpu
from jax.sharding import PartitionSpec as P

STEP = 10


beta_one = 0.9
beta_two = 0.999
adam_epsilon = 1e-08
learn_rate = 0.02
clip_limit = 16.0

RING = 8
ORDER = (4, 3, 5, 2, 6, 1, 7)
MESH = pl.DeviceIdType.MESH
HIGH = lax.Precision.HIGHEST
F32 = jnp.float32
BF16 = jnp.bfloat16


def dot_nn(a, b):
    return lax.dot_general(a, b, (((1,), (0,)), ((), ())), precision=HIGH, preferred_element_type=F32)


def dot_tn(a, b):
    return lax.dot_general(a, b, (((0,), (0,)), ((), ())), precision=HIGH, preferred_element_type=F32)


def dot_nt(a, b):
    return lax.dot_general(a, b, (((1,), (1,)), ((), ())), precision=HIGH, preferred_element_type=F32)


def three_parts(value):
    high = value.astype(BF16)
    rest = value - high.astype(F32)
    middle = rest.astype(BF16)
    low = (rest - middle.astype(F32)).astype(BF16)
    return high, middle, low


def lower_inverse(gram):
    rank = gram.shape[0]
    rows = lax.broadcasted_iota(jnp.int32, (rank, 128), 0)
    lanes = lax.broadcasted_iota(jnp.int32, (rank, 128), 1)
    identity = jnp.where(lanes == rows + rank, 1.0, 0.0).astype(F32)
    wide = jnp.concatenate([gram, jnp.zeros((rank, 128 - rank), F32)], axis=1) + identity
    pivots = jnp.ones((rank, 128), F32)
    for k in range(rank):
        column = jnp.broadcast_to(wide[:, k : k + 1], (rank, 128))
        pivot = jnp.broadcast_to(column[k : k + 1, :], (rank, 128))
        row = jnp.broadcast_to(wide[k : k + 1, :], (rank, 128))
        pivots = jnp.where(rows == k, pivot, pivots)
        factor = jnp.where(rows > k, column / pivot, 0.0)
        wide = wide - factor * row
    scaled = wide * lax.rsqrt(pivots)
    return scaled[:, rank : 2 * rank]


def step_kernel(
    g_ref, e_ref, q_ref, master_ref, first_ref, second_ref,
    err_ref, right_ref, new_master_ref, new_first_ref, new_second_ref, out_ref,
    local, red_a, red_b, sum_a, sum_b, full, fold, fold_a, fold_b, next_a, next_b, norm, norms,
    group, send_a, send_b, gat_a, gat_b, nat_a, tail_b, ss, rs,
):
    section = lax.axis_index("section")
    dp = lax.axis_index("dp")
    y = lax.div(dp, RING)
    z = lax.rem(dp, RING)
    replicas = RING * RING
    rank = q_ref.shape[0]
    half = rank // 2
    width = g_ref.shape[1] // RING
    owned = master_ref.shape[0]

    def up(i, d):
        return lax.rem(i + d, RING)

    def down(i, d):
        return lax.rem(i + RING - d, RING)

    def peer(axis, d):
        if axis == "z":
            return (section, y * RING + up(z, d))
        if axis == "y":
            return (section, up(y, d) * RING + z)
        return (up(section, d), dp)

    def copy(phase, lane, axis, d, src, dst):
        return pltpu.make_async_remote_copy(
            src_ref=src, dst_ref=dst, send_sem=ss.at[phase, lane, d], recv_sem=rs.at[phase, lane, d],
            device_id=peer(axis, d), device_id_type=MESH,
        )

    barrier = pltpu.get_barrier_semaphore()
    for axis in ("z", "y", "s"):
        for d in range(1, RING):
            pl.semaphore_signal(barrier, 1, device_id=peer(axis, d), device_id_type=MESH)

    parts = jnp.concatenate(three_parts(q_ref[...]), axis=0)
    for j in range(RING):
        cols = pl.ds(j * width, width)
        term = jnp.dot(parts, g_ref[:, cols], preferred_element_type=F32)
        term += jnp.dot(parts, e_ref[:, cols], preferred_element_type=F32)
        local[j] = term[:rank] + term[rank : 2 * rank] + term[2 * rank :]

    pl.semaphore_wait(barrier, 3 * (RING - 1))

    started = []

    def send(*args):
        c = copy(*args)
        c.start()
        started.append(c)

    for d in ORDER:
        send(0, 0, "z", d, local.at[up(z, d), pl.ds(0, half)], red_a.at[d - 1])
        send(0, 1, "y", d, local.at[up(y, d), pl.ds(half, half)], red_b.at[d - 1])
    total_a = local[z, 0:half]
    total_b = local[y, half:rank]
    for d in ORDER[::-1]:
        copy(0, 0, "z", d, red_a.at[d - 1], red_a.at[d - 1]).wait_recv()
        total_a += red_a[d - 1]
        copy(0, 1, "y", d, red_b.at[d - 1], red_b.at[d - 1]).wait_recv()
        total_b += red_b[d - 1]
    sum_a[y] = total_a
    sum_b[z] = total_b
    for d in ORDER:
        send(1, 0, "y", d, sum_a.at[y], sum_a.at[y])
        send(1, 1, "z", d, sum_b.at[z], sum_b.at[z])
    for d in ORDER[::-1]:
        copy(1, 0, "y", d, sum_a.at[down(y, d)], sum_a.at[down(y, d)]).wait_recv()
        copy(1, 1, "z", d, sum_b.at[down(z, d)], sum_b.at[down(z, d)]).wait_recv()
    total_a = sum_a[0]
    total_b = sum_b[0]
    for i in range(1, RING):
        total_a += sum_a[i]
        total_b += sum_b[i]
    full[z, 0:half] = total_a
    full[y, half:rank] = total_b
    for d in ORDER:
        send(2, 0, "z", d, full.at[z, pl.ds(0, half)], full.at[z, pl.ds(0, half)])
        send(2, 1, "y", d, full.at[y, pl.ds(half, half)], full.at[y, pl.ds(half, half)])
    for d in ORDER[::-1]:
        src_z, src_y = down(z, d), down(y, d)
        copy(2, 0, "z", d, full.at[src_z, pl.ds(0, half)], full.at[src_z, pl.ds(0, half)]).wait_recv()
        copy(2, 1, "y", d, full.at[src_y, pl.ds(half, half)], full.at[src_y, pl.ds(half, half)]).wait_recv()

    right = jnp.zeros((3 * rank, g_ref.shape[0]), F32)
    for j in range(RING):
        cols = pl.ds(j * width, width)
        parts = jnp.concatenate(three_parts(full[j]), axis=0)
        for source in (g_ref, e_ref):
            right += lax.dot_general(
                parts, source[:, cols], (((1,), (1,)), ((), ())), preferred_element_type=F32
            )
    right = right[:rank] + right[rank : 2 * rank] + right[2 * rank :]
    rest = jnp.concatenate([right[:half, 128:192], right[half:, 128:192]], axis=1)
    fold[0:16] = right[:half, :128]
    fold[16:24] = rest[:8]
    fold[24:40] = right[half:, :128]
    fold[40:48] = rest[8:]
    fold_a[z] = fold[0:24]
    fold_b[y] = fold[24:48]
    for d in ORDER:
        send(3, 0, "z", d, fold_a.at[z], fold_a.at[z])
        send(3, 1, "y", d, fold_b.at[y], fold_b.at[y])

    gram = jnp.zeros((rank, rank), F32)
    for j in range(RING):
        gram += dot_nt(full[j], full[j])
    inverse = lower_inverse(gram)

    for d in ORDER[::-1]:
        copy(3, 0, "z", d, fold_a.at[down(z, d)], fold_a.at[down(z, d)]).wait_recv()
        copy(3, 1, "y", d, fold_b.at[down(y, d)], fold_b.at[down(y, d)]).wait_recv()
    total_a = fold_a[0]
    total_b = fold_b[0]
    for i in range(1, RING):
        total_a += fold_a[i]
        total_b += fold_b[i]
    next_a[y] = total_a
    next_b[z] = total_b
    for d in ORDER:
        send(4, 0, "y", d, next_a.at[y], next_a.at[y])
        send(4, 1, "z", d, next_b.at[z], next_b.at[z])
    for d in ORDER[::-1]:
        copy(4, 0, "y", d, next_a.at[down(y, d)], next_a.at[down(y, d)]).wait_recv()
        copy(4, 1, "z", d, next_b.at[down(z, d)], next_b.at[down(z, d)]).wait_recv()
    total_a = next_a[0]
    total_b = next_b[0]
    for i in range(1, RING):
        total_a += next_a[i]
        total_b += next_b[i]
    rest = jnp.concatenate([total_a[16:24], total_b[16:24]], axis=0)
    top = jnp.concatenate([total_a[0:16], total_b[0:16]], axis=0)
    rest = jnp.concatenate([rest[:, :64], rest[:, 64:]], axis=0)
    right = jnp.concatenate([top, rest], axis=1)
    right = dot_nn(inverse, right) * (1.0 / replicas)
    right_ref[...] = right
    squares = jnp.sum(right * right, keepdims=True)
    norms[section] = jnp.broadcast_to(squares, (8, 128))
    for d in ORDER:
        send(5, 0, "s", d, norms.at[section], norms.at[section])

    coef = dot_tn(inverse, right)
    group[...] = dot_tn(full[y], coef)
    grad = group[pl.ds(pl.multiple_of(z * owned, 8), owned)]

    for d in ORDER[::-1]:
        copy(5, 0, "s", d, norms.at[down(section, d)], norms.at[down(section, d)]).wait_recv()
    squares = norms[0]
    for i in range(1, RING):
        squares += norms[i]
    clip = jnp.minimum(1.0, clip_limit / jnp.sqrt(squares))[0:1, 0:1]
    scaled = clip * grad
    new_first = beta_one * first_ref[...] + (1.0 - beta_one) * scaled
    new_second = beta_two * second_ref[...] + (1.0 - beta_two) * scaled * scaled
    adam_step = (
        new_first
        / (1.0 - beta_one**STEP)
        / (jnp.sqrt(new_second / (1.0 - beta_two**STEP)) + adam_epsilon)
    )
    new_master = master_ref[...] - learn_rate * adam_step
    new_first_ref[...] = new_first
    new_second_ref[...] = new_second
    new_master_ref[...] = new_master
    short = new_master.astype(BF16)
    gat_a[z] = short[:, 0:128]
    gat_b[y] = short[:, 64:192]
    for d in ORDER:
        send(6, 0, "z", d, gat_a.at[z], gat_a.at[z])
        send(6, 1, "y", d, gat_b.at[y], gat_b.at[y])
    for d in ORDER[::-1]:
        copy(6, 0, "z", d, gat_a.at[down(z, d)], gat_a.at[down(z, d)]).wait_recv()
        copy(6, 1, "y", d, gat_b.at[down(y, d)], gat_b.at[down(y, d)]).wait_recv()
    rows = g_ref.shape[0] // 2
    mine = pl.ds(pl.multiple_of(y * width, 128), width)
    out_ref[0:rows, mine] = gat_a[...].reshape(width, 128).T[0:rows]
    tail_b[z] = gat_b[...]
    for d in ORDER:
        here = out_ref.at[pl.ds(0, rows), mine]
        send(7, 0, "y", d, here, here)
        send(7, 1, "z", d, tail_b.at[z], tail_b.at[z])

    high, low, _ = three_parts(coef)
    left = jnp.concatenate([high, high, low], axis=0)
    for j in range(RING):
        cols = pl.ds(j * width, width)
        high, low, _ = three_parts(full[j])
        approx = lax.dot_general(
            left, jnp.concatenate([high, low, high], axis=0), (((0,), (0,)), ((), ())),
            preferred_element_type=F32,
        )
        combined = g_ref[:, cols].astype(F32) + e_ref[:, cols].astype(F32)
        err_ref[:, cols] = (combined - approx).astype(BF16)

    for d in ORDER[::-1]:
        copy(7, 1, "z", d, tail_b.at[down(z, d)], tail_b.at[down(z, d)]).wait_recv()
    for j in range(RING):
        block = tail_b[:, j].reshape(width, 128)
        out_ref[rows:, j * width : (j + 1) * width] = block.T[128 - rows :]
    for d in ORDER[::-1]:
        there = out_ref.at[pl.ds(0, rows), pl.ds(pl.multiple_of(down(y, d) * width, 128), width)]
        copy(7, 0, "y", d, there, there).wait_recv()
    for c in started:
        c.wait_send()


def per_device(gradients, error_buffers, initial_q, master, first_moment, second_moment):
    rows, cols = gradients.shape[2:]
    rank = initial_q.shape[2]
    owned = master.shape[2]
    half = rank // 2
    width = cols // RING
    vmem = pl.BlockSpec(memory_space=pltpu.VMEM)
    outs = pl.pallas_call(
        step_kernel,
        name="relay_step",
        out_shape=(
            jax.ShapeDtypeStruct((rows, cols), BF16),
            jax.ShapeDtypeStruct((rank, rows), F32),
            jax.ShapeDtypeStruct((owned, rows), F32),
            jax.ShapeDtypeStruct((owned, rows), F32),
            jax.ShapeDtypeStruct((owned, rows), F32),
            jax.ShapeDtypeStruct((rows, cols), BF16),
        ),
        in_specs=[vmem] * 6,
        out_specs=(vmem,) * 6,
        scratch_shapes=[
            pltpu.VMEM((RING, rank, width), F32),
            pltpu.VMEM((RING - 1, half, width), F32),
            pltpu.VMEM((RING - 1, half, width), F32),
            pltpu.VMEM((RING, half, width), F32),
            pltpu.VMEM((RING, half, width), F32),
            pltpu.VMEM((RING, rank, width), F32),
            pltpu.VMEM((48, 128), F32),
            pltpu.VMEM((RING, 24, 128), F32),
            pltpu.VMEM((RING, 24, 128), F32),
            pltpu.VMEM((RING, 24, 128), F32),
            pltpu.VMEM((RING, 24, 128), F32),
            pltpu.VMEM((8, 128), F32),
            pltpu.VMEM((RING, 8, 128), F32),
            pltpu.VMEM((width, rows), F32),
            pltpu.VMEM((owned, 128), BF16),
            pltpu.VMEM((owned, 128), BF16),
            pltpu.VMEM((RING, owned, 128), BF16),
            pltpu.VMEM((RING, owned, 128), BF16),
            pltpu.VMEM((rows // 2, width), BF16),
            pltpu.VMEM((RING, RING, owned, 128), BF16),
            pltpu.SemaphoreType.DMA((8, 2, RING)),
            pltpu.SemaphoreType.DMA((8, 2, RING)),
        ],
        compiler_params=pltpu.CompilerParams(
            collective_id=0, has_side_effects=True, vmem_limit_bytes=40 << 20
        ),
    )(
        gradients[0, 0],
        error_buffers[0, 0],
        initial_q[0].T,
        master[0].T,
        first_moment[0].T,
        second_moment[0].T,
    )
    new_errors, right, new_master, new_first, new_second, gathered = outs
    return (
        new_errors[None, None],
        right.T[None],
        new_master.T[None],
        new_first.T[None],
        new_second.T[None],
        gathered[None],
    )


def solution(mesh):
    placed = (
        P("section", "dp", None, None),
        P("section", "dp", None, None),
        P("section", None, None),
        P("section", None, "dp"),
        P("section", None, "dp"),
        P("section", None, "dp"),
    )
    return jax.shard_map(
        per_device,
        mesh=mesh,
        in_specs=placed,
        out_specs=(
            P("section", "dp", None, None),
            P("section", None, None),
            P("section", None, "dp"),
            P("section", None, "dp"),
            P("section", None, "dp"),
            P("section", None, None),
        ),
        check_vma=False,
    )
```

```python
import functools

import jax
import jax.numpy as jnp
from jax import lax
from jax.experimental import pallas as pl
from jax.experimental.pallas import tpu as pltpu
from jax.sharding import PartitionSpec as P

STEP = 10


beta_one = 0.9
beta_two = 0.999
adam_epsilon = 1e-08
learn_rate = 0.02
clip_limit = 16.0

RING = 8
ORDER = (4, 3, 5, 2, 6, 1, 7)
MESH = pl.DeviceIdType.MESH
HIGH = lax.Precision.HIGHEST
F32 = jnp.float32
BF16 = jnp.bfloat16


def dot_nn(a, b):
    return lax.dot_general(a, b, (((1,), (0,)), ((), ())), precision=HIGH, preferred_element_type=F32)


def dot_tn(a, b):
    return lax.dot_general(a, b, (((0,), (0,)), ((), ())), precision=HIGH, preferred_element_type=F32)


def dot_nt(a, b):
    return lax.dot_general(a, b, (((1,), (1,)), ((), ())), precision=HIGH, preferred_element_type=F32)


def three_parts(value):
    high = value.astype(BF16)
    rest = value - high.astype(F32)
    middle = rest.astype(BF16)
    low = (rest - middle.astype(F32)).astype(BF16)
    return high, middle, low


def widen(gram):
    rank = gram.shape[0]
    rows = lax.broadcasted_iota(jnp.int32, (rank, 128), 0)
    lanes = lax.broadcasted_iota(jnp.int32, (rank, 128), 1)
    identity = jnp.where(lanes == rows + rank, 1.0, 0.0).astype(F32)
    wide = jnp.concatenate([gram, jnp.zeros((rank, 128 - rank), F32)], axis=1) + identity
    return wide, jnp.ones((rank, 128), F32)


def eliminate(state, first, last):
    wide, pivots = state
    rank = wide.shape[0]
    rows = lax.broadcasted_iota(jnp.int32, (rank, 128), 0)
    for k in range(first, last):
        column = jnp.broadcast_to(wide[:, k : k + 1], (rank, 128))
        pivot = jnp.broadcast_to(column[k : k + 1, :], (rank, 128))
        row = jnp.broadcast_to(wide[k : k + 1, :], (rank, 128))
        pivots = jnp.where(rows == k, pivot, pivots)
        factor = jnp.where(rows > k, column / pivot, 0.0)
        wide = wide - factor * row
    return wide, pivots


def step_kernel(
    g_hbm, e_hbm, q_hbm, master_hbm, first_hbm, second_hbm,
    err_ref, right_ref, new_master_ref, new_first_ref, new_second_ref, out_ref,
    g_ref, e_ref, q_ref, states, local, red_a, red_b, sum_a, sum_b, full, fold_a, fold_b, next_a, next_b,
    norms, pre_a, pre_b, grad_a, grad_b, tail_b, loads, ss, rs,
):
    section = lax.axis_index("section")
    dp = lax.axis_index("dp")
    y = lax.div(dp, RING)
    z = lax.rem(dp, RING)
    replicas = RING * RING
    rank = q_ref.shape[0]
    half = rank // 2
    width = g_ref.shape[1] // RING
    owned = master_hbm.shape[0]
    rows = g_ref.shape[0] // 2

    def up(i, d):
        return lax.rem(i + d, RING)

    def down(i, d):
        return lax.rem(i + RING - d, RING)

    def peer(axis, d):
        if axis == "z":
            return (section, y * RING + up(z, d))
        if axis == "y":
            return (section, up(y, d) * RING + z)
        return (up(section, d), dp)

    def remote(phase, lane, sem, axis, d, src, dst):
        return pltpu.make_async_remote_copy(
            src_ref=src, dst_ref=dst, send_sem=ss.at[phase, lane, sem], recv_sem=rs.at[phase, lane, sem],
            device_id=peer(axis, d), device_id_type=MESH,
        )

    def copy(phase, lane, axis, d, src, dst):
        return remote(phase, lane, d, axis, d, src, dst)

    started = []

    def send(*args):
        c = copy(*args)
        c.start()
        started.append(c)

    barrier = pltpu.get_barrier_semaphore()
    for axis in ("z", "y", "s"):
        for d in range(1, RING):
            pl.semaphore_signal(barrier, 1, device_id=peer(axis, d), device_id_type=MESH)

    sources = [(q_hbm, q_ref), (g_hbm, g_ref), (e_hbm, e_ref)]
    sources += [(x, states.at[i]) for i, x in enumerate((first_hbm, second_hbm, master_hbm))]
    fetch = [pltpu.make_async_copy(x, v, loads.at[i]) for i, (x, v) in enumerate(sources)]
    for c in fetch:
        c.start()
    for c in fetch[:3]:
        c.wait()

    parts = jnp.concatenate(three_parts(q_ref[...]), axis=0)
    for j in range(RING):
        cols = pl.ds(j * width, width)
        term = jnp.dot(parts, g_ref[:, cols], preferred_element_type=F32)
        term += jnp.dot(parts, e_ref[:, cols], preferred_element_type=F32)
        local[j] = term[:rank] + term[rank : 2 * rank] + term[2 * rank :]
    for c in fetch[3:]:
        c.wait()
    for i in range(3):
        value = states[i]
        pre_a[z, i] = value[:, :128]
        pre_b[y, i] = jnp.concatenate([value[:, rows:], value[:, : 128 - rows]], axis=1)

    pl.semaphore_wait(barrier, 3 * (RING - 1))

    def state_copy(lane, step, way):
        axis, place, buf = (("z", z, pre_a), ("y", y, pre_b))[lane]
        block = down(place, step - 1) if way == 0 else up(place, step - 1)
        view = buf.at[block]
        if step == RING // 2:
            part = owned // 2
            view = buf.at[block, :, pl.ds(part * way, part)]
        return remote(6, lane, way * 4 + step - 1, axis, 1 if way == 0 else RING - 1, view, view)

    def state_landed(lane, step, way):
        axis, place, buf = (("z", z, pre_a), ("y", y, pre_b))[lane]
        block = down(place, step) if way == 0 else up(place, step)
        view = buf.at[block]
        if step == RING // 2:
            part = owned // 2
            view = buf.at[block, :, pl.ds(part * way, part)]
        return remote(6, lane, way * 4 + step - 1, axis, 1 if way == 0 else RING - 1, view, view)

    def state_step(step):
        for lane in range(2):
            for way in range(2):
                if step > 1:
                    state_landed(lane, step - 1, way).wait_recv()
                if step <= RING // 2:
                    c = state_copy(lane, step, way)
                    c.start()
                    started.append(c)

    for d in ORDER:
        send(0, 0, "z", d, local.at[up(z, d), pl.ds(0, half)], red_a.at[d - 1])
        send(0, 1, "y", d, local.at[up(y, d), pl.ds(half, half)], red_b.at[d - 1])
    state_step(1)
    total_a = local[z, 0:half]
    total_b = local[y, half:rank]
    for d in ORDER[::-1]:
        copy(0, 0, "z", d, red_a.at[d - 1], red_a.at[d - 1]).wait_recv()
        total_a += red_a[d - 1]
        copy(0, 1, "y", d, red_b.at[d - 1], red_b.at[d - 1]).wait_recv()
        total_b += red_b[d - 1]
    sum_a[y] = total_a
    sum_b[z] = total_b
    for d in ORDER:
        send(1, 0, "y", d, sum_a.at[y], sum_a.at[y])
        send(1, 1, "z", d, sum_b.at[z], sum_b.at[z])
    state_step(2)
    for d in ORDER[::-1]:
        copy(1, 0, "y", d, sum_a.at[down(y, d)], sum_a.at[down(y, d)]).wait_recv()
        copy(1, 1, "z", d, sum_b.at[down(z, d)], sum_b.at[down(z, d)]).wait_recv()
    total_a = sum_a[0]
    total_b = sum_b[0]
    for i in range(1, RING):
        total_a += sum_a[i]
        total_b += sum_b[i]
    full[z, 0:half] = total_a
    full[y, half:rank] = total_b
    for d in ORDER:
        send(2, 0, "z", d, full.at[z, pl.ds(0, half)], full.at[z, pl.ds(0, half)])
        send(2, 1, "y", d, full.at[y, pl.ds(half, half)], full.at[y, pl.ds(half, half)])
    state_step(3)
    for d in ORDER[::-1]:
        src_z, src_y = down(z, d), down(y, d)
        copy(2, 0, "z", d, full.at[src_z, pl.ds(0, half)], full.at[src_z, pl.ds(0, half)]).wait_recv()
        copy(2, 1, "y", d, full.at[src_y, pl.ds(half, half)], full.at[src_y, pl.ds(half, half)]).wait_recv()

    right = jnp.zeros((3 * rank, g_ref.shape[0]), F32)
    for j in range(RING):
        cols = pl.ds(j * width, width)
        parts = jnp.concatenate(three_parts(full[j]), axis=0)
        for source in (g_ref, e_ref):
            right += lax.dot_general(
                parts, source[:, cols], (((1,), (1,)), ((), ())), preferred_element_type=F32
            )
    right = right[:rank] + right[rank : 2 * rank] + right[2 * rank :]
    rest = jnp.concatenate([right[:half, 128:192], right[half:, 128:192]], axis=1)
    fold_a[z, 0:16] = right[:half, :128]
    fold_a[z, 16:24] = rest[:8]
    fold_b[y, 0:16] = right[half:, :128]
    fold_b[y, 16:24] = rest[8:]
    for d in ORDER:
        send(3, 0, "z", d, fold_a.at[z], fold_a.at[z])
        send(3, 1, "y", d, fold_b.at[y], fold_b.at[y])
    state_step(4)

    gram = jnp.zeros((rank, rank), F32)
    for j in range(RING):
        gram += dot_nt(full[j], full[j])
    state = eliminate(widen(gram), 0, rank // 2)

    for d in ORDER[::-1]:
        copy(3, 0, "z", d, fold_a.at[down(z, d)], fold_a.at[down(z, d)]).wait_recv()
        copy(3, 1, "y", d, fold_b.at[down(y, d)], fold_b.at[down(y, d)]).wait_recv()
    total_a = fold_a[0]
    total_b = fold_b[0]
    for i in range(1, RING):
        total_a += fold_a[i]
        total_b += fold_b[i]
    next_a[y] = total_a
    next_b[z] = total_b
    for d in ORDER:
        send(4, 0, "y", d, next_a.at[y], next_a.at[y])
        send(4, 1, "z", d, next_b.at[z], next_b.at[z])

    wide, pivots = eliminate(state, rank // 2, rank)
    inverse = (wide * lax.rsqrt(pivots))[:, rank : 2 * rank]
    from_col = lax.broadcasted_iota(jnp.int32, (width, width), 0)
    to_col = lax.broadcasted_iota(jnp.int32, (width, width), 1)
    picked = jnp.zeros((3 * rank, width), F32)
    for i in range(RING):
        chosen = jnp.where(
            (from_col - owned * z == to_col - owned * i) & (to_col >= owned * i) & (to_col < owned * (i + 1)),
            1.0, 0.0,
        ).astype(BF16)
        parts = jnp.concatenate(three_parts(full[i]), axis=0)
        picked += jnp.dot(parts, chosen, preferred_element_type=F32)
    picked = picked[:rank] + picked[rank : 2 * rank] + picked[2 * rank :]

    for d in ORDER[::-1]:
        copy(4, 0, "y", d, next_a.at[down(y, d)], next_a.at[down(y, d)]).wait_recv()
        copy(4, 1, "z", d, next_b.at[down(z, d)], next_b.at[down(z, d)]).wait_recv()
    total_a = next_a[0]
    total_b = next_b[0]
    for i in range(1, RING):
        total_a += next_a[i]
        total_b += next_b[i]
    rest = jnp.concatenate([total_a[16:24], total_b[16:24]], axis=0)
    top = jnp.concatenate([total_a[0:16], total_b[0:16]], axis=0)
    rest = jnp.concatenate([rest[:, :64], rest[:, 64:]], axis=0)
    right = jnp.concatenate([top, rest], axis=1)
    right = dot_nn(inverse, right) * (1.0 / replicas)
    squares = jnp.sum(right * right, keepdims=True)
    norms[section] = jnp.broadcast_to(squares, (8, 128))
    for d in ORDER:
        send(5, 0, "s", d, norms.at[section], norms.at[section])
    right_ref[...] = right
    state_step(5)

    coef = dot_tn(inverse, right)
    grad_a[...] = dot_tn(full[y], coef[:, :128])
    grad_b[...] = dot_tn(picked, jnp.concatenate([coef[:, rows:], coef[:, : 128 - rows]], axis=1))
    high, low, _ = three_parts(coef)
    left = jnp.concatenate([high, high, low], axis=0)
    for j in range(RING):
        cols = pl.ds(j * width, width)
        high, low, _ = three_parts(full[j])
        approx = lax.dot_general(
            left, jnp.concatenate([high, low, high], axis=0), (((0,), (0,)), ((), ())),
            preferred_element_type=F32,
        )
        combined = g_ref[:, cols].astype(F32) + e_ref[:, cols].astype(F32)
        err_ref[:, cols] = (combined - approx).astype(BF16)

    for d in ORDER[::-1]:
        copy(5, 0, "s", d, norms.at[down(section, d)], norms.at[down(section, d)]).wait_recv()
    squares = norms[0]
    for i in range(1, RING):
        squares += norms[i]
    clip = jnp.minimum(1.0, clip_limit / jnp.sqrt(squares))[0:1, 0:1]

    def update(grad, first, second, master):
        scaled = clip * grad
        new_first = beta_one * first + (1.0 - beta_one) * scaled
        new_second = beta_two * second + (1.0 - beta_two) * scaled * scaled
        adam_step = (
            new_first
            / (1.0 - beta_one**STEP)
            / (jnp.sqrt(new_second / (1.0 - beta_two**STEP)) + adam_epsilon)
        )
        return master - learn_rate * adam_step, new_first, new_second

    def group_update(grad, buf):
        first, second, master = (buf[:, i].reshape(width, 128) for i in range(3))
        return update(grad, first, second, master)[0]

    mine = pl.ds(pl.multiple_of(y * width, 128), width)
    out_ref[0:rows, mine] = group_update(grad_a[...], pre_a).astype(BF16).T[0:rows]

    def weight_copy(lane, sem, here, there):
        axis, place = (("y", y), ("z", z))[lane]
        part, d = (
            (None, 2), (None, RING - 2), (None, 1), (None, RING - 1),
            (0, 2), (None, 1), (1, RING - 2), (None, RING - 1),
        )[sem]

        def view(block):
            if lane == 0:
                lanes = pl.ds(pl.multiple_of(block * width, 128), width)
                if part is None:
                    return out_ref.at[pl.ds(0, rows), lanes]
                return out_ref.at[pl.ds(part * (rows // 2), rows // 2), lanes]
            if part is None:
                return tail_b.at[block]
            return tail_b.at[block, pl.ds(3 * part, 3)]

        return remote(7, lane, sem, axis, d, view(here), view(there))

    def weight_start(lane, sem):
        place = (y, z)[lane]
        block = (place, place, place, place, down(place, 2), down(place, 2), up(place, 2), up(place, 2))[sem]
        c = weight_copy(lane, sem, block, block)
        c.start()
        started.append(c)

    def weight_landed(lane, sem):
        place = (y, z)[lane]
        block = (
            down(place, 2), up(place, 2), down(place, 1), up(place, 1),
            down(place, 4), down(place, 3), up(place, 4), up(place, 3),
        )[sem]
        weight_copy(lane, sem, block, block).wait_recv()

    for sem in range(4):
        weight_start(0, sem)
    tail = group_update(grad_b[...], pre_b)
    lanes = lax.broadcasted_iota(jnp.int32, (owned, 128), 1)
    for i in range(6):
        other = tail[(6 + i % 2) * owned : (7 + i % 2) * owned]
        shift = rows - 32 * (i // 2)
        other = jnp.concatenate([other[:, 128 - shift :], other[:, : 128 - shift]], axis=1)
        tail_b[z, i] = jnp.where(lanes < rows, tail[i * owned : (i + 1) * owned], other).astype(BF16)
    for sem in range(4):
        weight_start(1, sem)

    own_a = grad_a[pl.ds(pl.multiple_of(z * owned, 8), owned)]
    own_b = grad_b[pl.ds(pl.multiple_of(y * owned, 8), owned)]
    grad = jnp.concatenate([own_a[:, :rows], own_b[:, :rows]], axis=1)
    new_master, new_first, new_second = update(grad, states[0], states[1], states[2])
    new_master_ref[...] = new_master
    new_first_ref[...] = new_first
    new_second_ref[...] = new_second

    for sem in (0, 1):
        for lane in (0, 1):
            weight_landed(lane, sem)
            weight_start(lane, 4 + 2 * sem)
            weight_start(lane, 5 + 2 * sem)
    for sem in range(2, 8):
        weight_landed(1, sem)
    for i in range(6):
        block = tail_b[:, i].reshape(width, 128).T
        out_ref[rows:, i * width : (i + 1) * width] = block[:rows]
        first_row = rows + 32 * (i // 2)
        first_col = (6 + i % 2) * width
        out_ref[first_row : first_row + 32, first_col : first_col + width] = block[rows:]
    for sem in range(2, 8):
        weight_landed(0, sem)
    for c in started:
        c.wait_send()


def finish_kernel(*refs):
    sources, targets, sems = refs[:6], refs[6:12], refs[12]
    copies = [pltpu.make_async_copy(s, t, sems.at[i]) for i, (s, t) in enumerate(zip(sources, targets))]
    for c in copies:
        c.start()
    for c in copies:
        c.wait()


def per_device(gradients, error_buffers, initial_q, master, first_moment, second_moment):
    rows, cols = gradients.shape[2:]
    rank = initial_q.shape[2]
    owned = master.shape[2]
    half = rank // 2
    width = cols // RING
    vmem = pl.BlockSpec(memory_space=pltpu.VMEM)
    hbm = pl.BlockSpec(memory_space=pltpu.HBM)
    shapes = (
        jax.ShapeDtypeStruct((rows, cols), BF16),
        jax.ShapeDtypeStruct((rank, rows), F32),
        jax.ShapeDtypeStruct((owned, rows), F32),
        jax.ShapeDtypeStruct((owned, rows), F32),
        jax.ShapeDtypeStruct((owned, rows), F32),
        jax.ShapeDtypeStruct((rows, cols), BF16),
    )
    operands = (gradients[0, 0], error_buffers[0, 0], initial_q[0].T)
    operands += (master[0].T, first_moment[0].T, second_moment[0].T)
    outs = pl.pallas_call(
        step_kernel,
        name="relay_step",
        out_shape=tuple(pltpu.VMEM(x.shape, x.dtype) for x in shapes),
        in_specs=[hbm] * 6,
        out_specs=(vmem,) * 6,
        scratch_shapes=[
            pltpu.VMEM((rows, cols), BF16),
            pltpu.VMEM((rows, cols), BF16),
            pltpu.VMEM((rank, rows), F32),
            pltpu.VMEM((3, owned, rows), F32),
            pltpu.VMEM((RING, rank, width), F32),
            pltpu.VMEM((RING - 1, half, width), F32),
            pltpu.VMEM((RING - 1, half, width), F32),
            pltpu.VMEM((RING, half, width), F32),
            pltpu.VMEM((RING, half, width), F32),
            pltpu.VMEM((RING, rank, width), F32),
            pltpu.VMEM((RING, 24, 128), F32),
            pltpu.VMEM((RING, 24, 128), F32),
            pltpu.VMEM((RING, 24, 128), F32),
            pltpu.VMEM((RING, 24, 128), F32),
            pltpu.VMEM((RING, 8, 128), F32),
            pltpu.VMEM((RING, 3, owned, 128), F32),
            pltpu.VMEM((RING, 3, owned, 128), F32),
            pltpu.VMEM((width, 128), F32),
            pltpu.VMEM((width, 128), F32),
            pltpu.VMEM((RING, 6, owned, 128), BF16),
            pltpu.SemaphoreType.DMA((6,)),
            pltpu.SemaphoreType.DMA((8, 2, RING)),
            pltpu.SemaphoreType.DMA((8, 2, RING)),
        ],
        compiler_params=pltpu.CompilerParams(
            collective_id=0, has_side_effects=True, vmem_limit_bytes=40 << 20
        ),
    )(*(pltpu.with_memory_space_constraint(x, pltpu.HBM) for x in operands))
    outs = pl.pallas_call(
        finish_kernel,
        name="finish",
        out_shape=shapes,
        in_specs=[vmem] * 6,
        out_specs=(hbm,) * 6,
        scratch_shapes=[pltpu.SemaphoreType.DMA((6,))],
    )(*(pltpu.with_memory_space_constraint(x, pltpu.VMEM) for x in outs))
    new_errors, right, new_master, new_first, new_second, gathered = outs
    return (
        new_errors[None, None],
        right.T[None],
        new_master.T[None],
        new_first.T[None],
        new_second.T[None],
        gathered[None],
    )


def solution(mesh):
    placed = (
        P("section", "dp", None, None),
        P("section", "dp", None, None),
        P("section", None, None),
        P("section", None, "dp"),
        P("section", None, "dp"),
        P("section", None, "dp"),
    )
    return jax.shard_map(
        per_device,
        mesh=mesh,
        in_specs=placed,
        out_specs=(
            P("section", "dp", None, None),
            P("section", None, None),
            P("section", None, "dp"),
            P("section", None, "dp"),
            P("section", None, "dp"),
            P("section", None, None),
        ),
        check_vma=False,
    )
```

```python
import functools

import jax
import jax.numpy as jnp
from jax import lax
from jax.experimental import pallas as pl
from jax.experimental.pallas import tpu as pltpu
from jax.sharding import PartitionSpec as P

STEP = 10


beta_one = 0.9
beta_two = 0.999
adam_epsilon = 1e-08
learn_rate = 0.02
clip_limit = 16.0

RING = 8
ORDER = (4, 3, 5, 2, 6, 1, 7)
MESH = pl.DeviceIdType.MESH
HIGH = lax.Precision.HIGHEST
F32 = jnp.float32
BF16 = jnp.bfloat16


def dot_nn(a, b):
    return lax.dot_general(a, b, (((1,), (0,)), ((), ())), precision=HIGH, preferred_element_type=F32)


def dot_tn(a, b):
    return lax.dot_general(a, b, (((0,), (0,)), ((), ())), precision=HIGH, preferred_element_type=F32)


def dot_nt(a, b):
    return lax.dot_general(a, b, (((1,), (1,)), ((), ())), precision=HIGH, preferred_element_type=F32)


def three_parts(value):
    high = value.astype(BF16)
    rest = value - high.astype(F32)
    middle = rest.astype(BF16)
    low = (rest - middle.astype(F32)).astype(BF16)
    return high, middle, low


def widen(gram):
    rank = gram.shape[0]
    rows = lax.broadcasted_iota(jnp.int32, (rank, 128), 0)
    lanes = lax.broadcasted_iota(jnp.int32, (rank, 128), 1)
    identity = jnp.where(lanes == rows + rank, 1.0, 0.0).astype(F32)
    wide = jnp.concatenate([gram, jnp.zeros((rank, 128 - rank), F32)], axis=1) + identity
    return wide, jnp.ones((rank, 128), F32)


def eliminate(state, first, last):
    wide, pivots = state
    rank = wide.shape[0]
    rows = lax.broadcasted_iota(jnp.int32, (rank, 128), 0)
    for k in range(first, last):
        column = jnp.broadcast_to(wide[:, k : k + 1], (rank, 128))
        pivot = jnp.broadcast_to(column[k : k + 1, :], (rank, 128))
        row = jnp.broadcast_to(wide[k : k + 1, :], (rank, 128))
        pivots = jnp.where(rows == k, pivot, pivots)
        factor = jnp.where(rows > k, column / pivot, 0.0)
        wide = wide - factor * row
    return wide, pivots


def step_kernel(
    g_hbm, e_hbm, q_hbm, master_hbm, first_hbm, second_hbm,
    err_ref, right_ref, new_master_ref, new_first_ref, new_second_ref, out_ref,
    g_ref, e_ref, q_ref, states, local, red_a, red_b, sum_a, sum_b, full, fold_a, fold_b, next_a, next_b,
    norms, pre_a, pre_b, grad_a, grad_b, tail_b, loads, ss, rs,
):
    section = lax.axis_index("section")
    dp = lax.axis_index("dp")
    y = lax.div(dp, RING)
    z = lax.rem(dp, RING)
    replicas = RING * RING
    rank = q_ref.shape[0]
    half = rank // 2
    width = g_ref.shape[1] // RING
    owned = master_hbm.shape[0]
    rows = g_ref.shape[0] // 2

    def up(i, d):
        return lax.rem(i + d, RING)

    def down(i, d):
        return lax.rem(i + RING - d, RING)

    def peer(axis, d):
        if axis == "z":
            return (section, y * RING + up(z, d))
        if axis == "y":
            return (section, up(y, d) * RING + z)
        return (up(section, d), dp)

    def remote(phase, lane, sem, axis, d, src, dst):
        return pltpu.make_async_remote_copy(
            src_ref=src, dst_ref=dst, send_sem=ss.at[phase, lane, sem], recv_sem=rs.at[phase, lane, sem],
            device_id=peer(axis, d), device_id_type=MESH,
        )

    def copy(phase, lane, axis, d, src, dst, chunk=0):
        return remote(phase, lane, d + RING * chunk, axis, d, src, dst)

    started = []

    def send(*args):
        c = copy(*args)
        c.start()
        started.append(c)

    barrier = pltpu.get_barrier_semaphore()
    for axis in ("z", "y", "s"):
        for d in range(1, RING):
            pl.semaphore_signal(barrier, 1, device_id=peer(axis, d), device_id_type=MESH)

    sources = [(q_hbm, q_ref)]
    for i in range(2):
        cols = pl.ds(i * (RING // 2) * width, (RING // 2) * width)
        sources += [(g_hbm.at[:, cols], g_ref.at[:, cols]), (e_hbm.at[:, cols], e_ref.at[:, cols])]
    sources += [(x, states.at[i]) for i, x in enumerate((first_hbm, second_hbm, master_hbm))]
    fetch = [pltpu.make_async_copy(x, v, loads.at[i]) for i, (x, v) in enumerate(sources)]
    for c in fetch:
        c.start()
    fetch[0].wait()

    parts = jnp.concatenate(three_parts(q_ref[...]), axis=0)
    for j in range(RING):
        if j % (RING // 2) == 0:
            for c in fetch[1 + j // 2 : 3 + j // 2]:
                c.wait()
        cols = pl.ds(j * width, width)
        term = jnp.dot(parts, g_ref[:, cols], preferred_element_type=F32)
        term += jnp.dot(parts, e_ref[:, cols], preferred_element_type=F32)
        local[j] = term[:rank] + term[rank : 2 * rank] + term[2 * rank :]
    for c in fetch[5:]:
        c.wait()
    for i in range(3):
        value = states[i]
        pre_a[z, i] = value[:, :128]
        pre_b[y, i] = jnp.concatenate([value[:, rows:], value[:, : 128 - rows]], axis=1)

    pl.semaphore_wait(barrier, 3 * (RING - 1))

    def state_copy(lane, step, way):
        axis, place, buf = (("z", z, pre_a), ("y", y, pre_b))[lane]
        block = down(place, step - 1) if way == 0 else up(place, step - 1)
        view = buf.at[block]
        if step == RING // 2:
            part = owned // 2
            view = buf.at[block, :, pl.ds(part * way, part)]
        return remote(6, lane, way * 4 + step - 1, axis, 1 if way == 0 else RING - 1, view, view)

    def state_landed(lane, step, way):
        axis, place, buf = (("z", z, pre_a), ("y", y, pre_b))[lane]
        block = down(place, step) if way == 0 else up(place, step)
        view = buf.at[block]
        if step == RING // 2:
            part = owned // 2
            view = buf.at[block, :, pl.ds(part * way, part)]
        return remote(6, lane, way * 4 + step - 1, axis, 1 if way == 0 else RING - 1, view, view)

    def state_step(step):
        for lane in range(2):
            for way in range(2):
                if step > 1:
                    state_landed(lane, step - 1, way).wait_recv()
                if step <= RING // 2:
                    c = state_copy(lane, step, way)
                    c.start()
                    started.append(c)

    step = half // 2
    chunks = range(2)

    def near(c):
        return pl.ds(c * step, step)

    def far(c):
        return pl.ds(half + c * step, step)

    for c in chunks:
        for d in ORDER:
            send(0, 0, "z", d, local.at[up(z, d), near(c)], red_a.at[d - 1, near(c)], c)
            send(0, 1, "y", d, local.at[up(y, d), far(c)], red_b.at[d - 1, near(c)], c)
    state_step(1)
    for c in chunks:
        total_a = local[z, near(c)]
        total_b = local[y, far(c)]
        for d in ORDER[::-1]:
            here = red_a.at[d - 1, near(c)]
            copy(0, 0, "z", d, here, here, c).wait_recv()
            total_a += here[...]
            here = red_b.at[d - 1, near(c)]
            copy(0, 1, "y", d, here, here, c).wait_recv()
            total_b += here[...]
        sum_a[y, near(c)] = total_a
        sum_b[z, near(c)] = total_b
        for d in ORDER:
            send(1, 0, "y", d, sum_a.at[y, near(c)], sum_a.at[y, near(c)], c)
            send(1, 1, "z", d, sum_b.at[z, near(c)], sum_b.at[z, near(c)], c)
    state_step(2)
    for c in chunks:
        for d in ORDER[::-1]:
            here = sum_a.at[down(y, d), near(c)]
            copy(1, 0, "y", d, here, here, c).wait_recv()
            here = sum_b.at[down(z, d), near(c)]
            copy(1, 1, "z", d, here, here, c).wait_recv()
        total_a = sum_a[0, near(c)]
        total_b = sum_b[0, near(c)]
        for i in range(1, RING):
            total_a += sum_a[i, near(c)]
            total_b += sum_b[i, near(c)]
        full[z, near(c)] = total_a
        full[y, far(c)] = total_b
        for d in ORDER:
            send(2, 0, "z", d, full.at[z, near(c)], full.at[z, near(c)], c)
            send(2, 1, "y", d, full.at[y, far(c)], full.at[y, far(c)], c)
    state_step(3)
    for c in chunks:
        for d in ORDER[::-1]:
            here = full.at[down(z, d), near(c)]
            copy(2, 0, "z", d, here, here, c).wait_recv()
            here = full.at[down(y, d), far(c)]
            copy(2, 1, "y", d, here, here, c).wait_recv()

    whole = jnp.concatenate([full[j] for j in range(RING)], axis=1)
    parts = jnp.concatenate(three_parts(whole), axis=0)
    right = sum(
        lax.dot_general(parts, source[...], (((1,), (1,)), ((), ())), preferred_element_type=F32)
        for source in (g_ref, e_ref)
    )
    right = right[:rank] + right[rank : 2 * rank] + right[2 * rank :]
    rest = jnp.concatenate([right[:half, 128:192], right[half:, 128:192]], axis=1)
    fold_a[z, 0:16] = right[:half, :128]
    fold_a[z, 16:24] = rest[:8]
    fold_b[y, 0:16] = right[half:, :128]
    fold_b[y, 16:24] = rest[8:]
    for d in ORDER:
        send(3, 0, "z", d, fold_a.at[z], fold_a.at[z])
        send(3, 1, "y", d, fold_b.at[y], fold_b.at[y])
    state_step(4)

    gram = jnp.zeros((rank, rank), F32)
    for j in range(RING):
        gram += dot_nt(full[j], full[j])
    state = eliminate(widen(gram), 0, rank // 2)

    for d in ORDER[::-1]:
        copy(3, 0, "z", d, fold_a.at[down(z, d)], fold_a.at[down(z, d)]).wait_recv()
        copy(3, 1, "y", d, fold_b.at[down(y, d)], fold_b.at[down(y, d)]).wait_recv()
    total_a = fold_a[0]
    total_b = fold_b[0]
    for i in range(1, RING):
        total_a += fold_a[i]
        total_b += fold_b[i]
    next_a[y] = total_a
    next_b[z] = total_b
    for d in ORDER:
        send(4, 0, "y", d, next_a.at[y], next_a.at[y])
        send(4, 1, "z", d, next_b.at[z], next_b.at[z])

    wide, pivots = eliminate(state, rank // 2, rank)
    inverse = (wide * lax.rsqrt(pivots))[:, rank : 2 * rank]
    from_col = lax.broadcasted_iota(jnp.int32, (width, width), 0)
    to_col = lax.broadcasted_iota(jnp.int32, (width, width), 1)
    picked = jnp.zeros((3 * rank, width), F32)
    for i in range(RING):
        chosen = jnp.where(
            (from_col - owned * z == to_col - owned * i) & (to_col >= owned * i) & (to_col < owned * (i + 1)),
            1.0, 0.0,
        ).astype(BF16)
        parts = jnp.concatenate(three_parts(full[i]), axis=0)
        picked += jnp.dot(parts, chosen, preferred_element_type=F32)
    picked = picked[:rank] + picked[rank : 2 * rank] + picked[2 * rank :]

    for d in ORDER[::-1]:
        copy(4, 0, "y", d, next_a.at[down(y, d)], next_a.at[down(y, d)]).wait_recv()
        copy(4, 1, "z", d, next_b.at[down(z, d)], next_b.at[down(z, d)]).wait_recv()
    total_a = next_a[0]
    total_b = next_b[0]
    for i in range(1, RING):
        total_a += next_a[i]
        total_b += next_b[i]
    rest = jnp.concatenate([total_a[16:24], total_b[16:24]], axis=0)
    top = jnp.concatenate([total_a[0:16], total_b[0:16]], axis=0)
    rest = jnp.concatenate([rest[:, :64], rest[:, 64:]], axis=0)
    right = jnp.concatenate([top, rest], axis=1)
    right = dot_nn(inverse, right) * (1.0 / replicas)
    squares = jnp.sum(right * right, keepdims=True)
    norms[section] = jnp.broadcast_to(squares, (8, 128))
    for d in ORDER:
        send(5, 0, "s", d, norms.at[section], norms.at[section])
    right_ref[...] = right
    state_step(5)

    coef = dot_tn(inverse, right)
    grad_a[...] = dot_tn(full[y], coef[:, :128])
    grad_b[...] = dot_tn(picked, jnp.concatenate([coef[:, rows:], coef[:, : 128 - rows]], axis=1))
    high, low, _ = three_parts(coef)
    left = jnp.concatenate([high, high, low], axis=0)
    for j in range(RING):
        cols = pl.ds(j * width, width)
        high, low, _ = three_parts(full[j])
        approx = lax.dot_general(
            left, jnp.concatenate([high, low, high], axis=0), (((0,), (0,)), ((), ())),
            preferred_element_type=F32,
        )
        combined = g_ref[:, cols].astype(F32) + e_ref[:, cols].astype(F32)
        err_ref[:, cols] = (combined - approx).astype(BF16)

    for d in ORDER[::-1]:
        copy(5, 0, "s", d, norms.at[down(section, d)], norms.at[down(section, d)]).wait_recv()
    squares = norms[0]
    for i in range(1, RING):
        squares += norms[i]
    clip = jnp.minimum(1.0, clip_limit / jnp.sqrt(squares))[0:1, 0:1]

    def update(grad, first, second, master):
        scaled = clip * grad
        new_first = beta_one * first + (1.0 - beta_one) * scaled
        new_second = beta_two * second + (1.0 - beta_two) * scaled * scaled
        adam_step = (
            new_first
            / (1.0 - beta_one**STEP)
            / (jnp.sqrt(new_second / (1.0 - beta_two**STEP)) + adam_epsilon)
        )
        return master - learn_rate * adam_step, new_first, new_second

    def group_update(grad, buf):
        first, second, master = (buf[:, i].reshape(width, 128) for i in range(3))
        return update(grad, first, second, master)[0]

    mine = pl.ds(pl.multiple_of(y * width, 128), width)
    out_ref[0:rows, mine] = group_update(grad_a[...], pre_a).astype(BF16).T[0:rows]

    hops = (
        (2, 0, 0), (-2, 0, 0), (2, 0, 1), (-2, 0, 1), (1, 0, 0), (-1, 0, 0), (1, 0, 1), (-1, 0, 1),
        (2, -2, 0), (1, -2, 0), (1, -2, 1), (-1, 2, 0), (-1, 2, 1), (-2, 2, 1),
    )

    def weight_copy(lane, sem, offset):
        axis, place = (("y", y), ("z", z))[lane]
        target, _, part = hops[sem]
        block = up(place, offset % RING)
        if lane == 0:
            lanes = pl.ds(pl.multiple_of(block * width, 128), width)
            view = out_ref.at[pl.ds(part * (rows // 2), rows // 2), lanes]
        else:
            view = tail_b.at[block, pl.ds(3 * part, 3)]
        return remote(7, lane, sem, axis, target % RING, view, view)

    def weight_start(lane, sem):
        c = weight_copy(lane, sem, hops[sem][1])
        c.start()
        started.append(c)

    def weight_landed(lane, sem):
        weight_copy(lane, sem, hops[sem][1] - hops[sem][0]).wait_recv()

    for sem in range(8):
        weight_start(0, sem)
    tail = group_update(grad_b[...], pre_b)
    lanes = lax.broadcasted_iota(jnp.int32, (owned, 128), 1)
    for i in range(6):
        other = tail[(6 + i % 2) * owned : (7 + i % 2) * owned]
        shift = rows - 32 * (i // 2)
        other = jnp.concatenate([other[:, 128 - shift :], other[:, : 128 - shift]], axis=1)
        tail_b[z, i] = jnp.where(lanes < rows, tail[i * owned : (i + 1) * owned], other).astype(BF16)
    for sem in range(8):
        weight_start(1, sem)

    own_a = grad_a[pl.ds(pl.multiple_of(z * owned, 8), owned)]
    own_b = grad_b[pl.ds(pl.multiple_of(y * owned, 8), owned)]
    grad = jnp.concatenate([own_a[:, :rows], own_b[:, :rows]], axis=1)
    new_master, new_first, new_second = update(grad, states[0], states[1], states[2])
    new_master_ref[...] = new_master
    new_first_ref[...] = new_first
    new_second_ref[...] = new_second

    for sem, onward in ((0, (8, 9)), (1, (11,)), (2, (10,)), (3, (13, 12))):
        for lane in (0, 1):
            weight_landed(lane, sem)
            for k in onward:
                weight_start(lane, k)
    for sem in range(4, 14):
        weight_landed(1, sem)
    for i in range(6):
        block = tail_b[:, i].reshape(width, 128).T
        out_ref[rows:, i * width : (i + 1) * width] = block[:rows]
        first_row = rows + 32 * (i // 2)
        first_col = (6 + i % 2) * width
        out_ref[first_row : first_row + 32, first_col : first_col + width] = block[rows:]
    for sem in range(4, 14):
        weight_landed(0, sem)
    for c in started:
        c.wait_send()


def finish_kernel(*refs):
    sources, targets, sems = refs[:6], refs[6:12], refs[12]
    copies = [pltpu.make_async_copy(s, t, sems.at[i]) for i, (s, t) in enumerate(zip(sources, targets))]
    for c in copies:
        c.start()
    for c in copies:
        c.wait()


def per_device(gradients, error_buffers, initial_q, master, first_moment, second_moment):
    rows, cols = gradients.shape[2:]
    rank = initial_q.shape[2]
    owned = master.shape[2]
    half = rank // 2
    width = cols // RING
    vmem = pl.BlockSpec(memory_space=pltpu.VMEM)
    hbm = pl.BlockSpec(memory_space=pltpu.HBM)
    shapes = (
        jax.ShapeDtypeStruct((rows, cols), BF16),
        jax.ShapeDtypeStruct((rank, rows), F32),
        jax.ShapeDtypeStruct((owned, rows), F32),
        jax.ShapeDtypeStruct((owned, rows), F32),
        jax.ShapeDtypeStruct((owned, rows), F32),
        jax.ShapeDtypeStruct((rows, cols), BF16),
    )
    operands = (gradients[0, 0], error_buffers[0, 0], initial_q[0].T)
    operands += (master[0].T, first_moment[0].T, second_moment[0].T)
    outs = pl.pallas_call(
        step_kernel,
        name="relay_step",
        out_shape=tuple(pltpu.VMEM(x.shape, x.dtype) for x in shapes),
        in_specs=[hbm] * 6,
        out_specs=(vmem,) * 6,
        scratch_shapes=[
            pltpu.VMEM((rows, cols), BF16),
            pltpu.VMEM((rows, cols), BF16),
            pltpu.VMEM((rank, rows), F32),
            pltpu.VMEM((3, owned, rows), F32),
            pltpu.VMEM((RING, rank, width), F32),
            pltpu.VMEM((RING - 1, half, width), F32),
            pltpu.VMEM((RING - 1, half, width), F32),
            pltpu.VMEM((RING, half, width), F32),
            pltpu.VMEM((RING, half, width), F32),
            pltpu.VMEM((RING, rank, width), F32),
            pltpu.VMEM((RING, 24, 128), F32),
            pltpu.VMEM((RING, 24, 128), F32),
            pltpu.VMEM((RING, 24, 128), F32),
            pltpu.VMEM((RING, 24, 128), F32),
            pltpu.VMEM((RING, 8, 128), F32),
            pltpu.VMEM((RING, 3, owned, 128), F32),
            pltpu.VMEM((RING, 3, owned, 128), F32),
            pltpu.VMEM((width, 128), F32),
            pltpu.VMEM((width, 128), F32),
            pltpu.VMEM((RING, 6, owned, 128), BF16),
            pltpu.SemaphoreType.DMA((8,)),
            pltpu.SemaphoreType.DMA((8, 2, 2 * RING)),
            pltpu.SemaphoreType.DMA((8, 2, 2 * RING)),
        ],
        compiler_params=pltpu.CompilerParams(
            collective_id=0, has_side_effects=True, vmem_limit_bytes=40 << 20
        ),
    )(*(pltpu.with_memory_space_constraint(x, pltpu.HBM) for x in operands))
    outs = pl.pallas_call(
        finish_kernel,
        name="finish",
        out_shape=shapes,
        in_specs=[vmem] * 6,
        out_specs=(hbm,) * 6,
        scratch_shapes=[pltpu.SemaphoreType.DMA((6,))],
    )(*(pltpu.with_memory_space_constraint(x, pltpu.VMEM) for x in outs))
    new_errors, right, new_master, new_first, new_second, gathered = outs
    return (
        new_errors[None, None],
        right.T[None],
        new_master.T[None],
        new_first.T[None],
        new_second.T[None],
        gathered[None],
    )


def solution(mesh):
    placed = (
        P("section", "dp", None, None),
        P("section", "dp", None, None),
        P("section", None, None),
        P("section", None, "dp"),
        P("section", None, "dp"),
        P("section", None, "dp"),
    )
    return jax.shard_map(
        per_device,
        mesh=mesh,
        in_specs=placed,
        out_specs=(
            P("section", "dp", None, None),
            P("section", None, None),
            P("section", None, "dp"),
            P("section", None, "dp"),
            P("section", None, "dp"),
            P("section", None, None),
        ),
        check_vma=False,
    )
```

```python
import functools

import jax
import jax.numpy as jnp
from jax import lax
from jax.experimental import pallas as pl
from jax.experimental.pallas import tpu as pltpu
from jax.sharding import PartitionSpec as P

STEP = 10


beta_one = 0.9
beta_two = 0.999
adam_epsilon = 1e-08
learn_rate = 0.02
clip_limit = 16.0

RING = 8
CHUNKS = 2
PIECES = 2
ORDER = (4, 3, 5, 2, 6, 1, 7)
MESH = pl.DeviceIdType.MESH
HIGH = lax.Precision.HIGHEST
F32 = jnp.float32
BF16 = jnp.bfloat16


def dot_nn(a, b):
    return lax.dot_general(a, b, (((1,), (0,)), ((), ())), precision=HIGH, preferred_element_type=F32)


def dot_tn(a, b):
    return lax.dot_general(a, b, (((0,), (0,)), ((), ())), precision=HIGH, preferred_element_type=F32)


def dot_nt(a, b):
    return lax.dot_general(a, b, (((1,), (1,)), ((), ())), precision=HIGH, preferred_element_type=F32)


def three_parts(value):
    high = value.astype(BF16)
    rest = value - high.astype(F32)
    middle = rest.astype(BF16)
    low = (rest - middle.astype(F32)).astype(BF16)
    return high, middle, low


def widen(gram):
    rank = gram.shape[0]
    rows = lax.broadcasted_iota(jnp.int32, (rank, 128), 0)
    lanes = lax.broadcasted_iota(jnp.int32, (rank, 128), 1)
    identity = jnp.where(lanes == rows + rank, 1.0, 0.0).astype(F32)
    wide = jnp.concatenate([gram, jnp.zeros((rank, 128 - rank), F32)], axis=1) + identity
    return wide, jnp.ones((rank, 128), F32)


def eliminate(state, first, last):
    wide, pivots = state
    rank = wide.shape[0]
    rows = lax.broadcasted_iota(jnp.int32, (rank, 128), 0)
    for k in range(first, last):
        column = jnp.broadcast_to(wide[:, k : k + 1], (rank, 128))
        pivot = jnp.broadcast_to(column[k : k + 1, :], (rank, 128))
        row = jnp.broadcast_to(wide[k : k + 1, :], (rank, 128))
        pivots = jnp.where(rows == k, pivot, pivots)
        factor = jnp.where(rows > k, column / pivot, 0.0)
        wide = wide - factor * row
    return wide, pivots


def step_kernel(
    g_hbm, e_hbm, q_hbm, master_hbm, first_hbm, second_hbm,
    err_ref, right_ref, new_master_ref, new_first_ref, new_second_ref, out_ref,
    g_ref, e_ref, q_ref, states, local, red_a, red_b, sum_a, sum_b, full, fold_a, fold_b, next_a, next_b,
    norms, pre_a, pre_b, grad_a, grad_b, tail_b, loads, sent, landed, state_sent, state_came, weight_sent, weight_came,
):
    section = lax.axis_index("section")
    dp = lax.axis_index("dp")
    y = lax.div(dp, RING)
    z = lax.rem(dp, RING)
    replicas = RING * RING
    rank = q_ref.shape[0]
    half = rank // 2
    width = g_ref.shape[1] // RING
    owned = master_hbm.shape[0]
    rows = g_ref.shape[0] // 2

    def up(i, d):
        return lax.rem(i + d, RING)

    def down(i, d):
        return lax.rem(i + RING - d, RING)

    def peer(axis, d):
        if axis == "z":
            return (section, y * RING + up(z, d))
        if axis == "y":
            return (section, up(y, d) * RING + z)
        return (up(section, d), dp)

    def remote(send_sem, recv_sem, axis, d, src, dst):
        return pltpu.make_async_remote_copy(
            src_ref=src, dst_ref=dst, send_sem=send_sem, recv_sem=recv_sem,
            device_id=peer(axis, d), device_id_type=MESH,
        )

    def slot(phase, lane, chunk):
        return (2 * phase + lane) * CHUNKS + chunk if phase < 3 else 6 * CHUNKS + 2 * (phase - 3) + lane

    def copy(phase, lane, axis, d, src, dst, chunk=0):
        k = slot(phase, lane, chunk)
        return remote(sent.at[k], landed.at[k], axis, d, src, dst)

    exchanges = []

    def send(*args):
        copy(*args).start()

    def gathered(phase, lane, view, chunk=0):
        c = copy(phase, lane, "z", 1, view, view, chunk)
        c.wait_recv()
        exchanges.append(c)

    barrier = pltpu.get_barrier_semaphore()
    for axis in ("z", "y", "s"):
        for d in range(1, RING):
            pl.semaphore_signal(barrier, 1, device_id=peer(axis, d), device_id_type=MESH)

    sources = [(q_hbm, q_ref)]
    for i in range(2):
        cols = pl.ds(i * (RING // 2) * width, (RING // 2) * width)
        sources += [(g_hbm.at[:, cols], g_ref.at[:, cols]), (e_hbm.at[:, cols], e_ref.at[:, cols])]
    sources += [(x, states.at[i]) for i, x in enumerate((first_hbm, second_hbm, master_hbm))]
    fetch = [pltpu.make_async_copy(x, v, loads.at[i]) for i, (x, v) in enumerate(sources)]
    for c in fetch:
        c.start()
    fetch[0].wait()

    parts = jnp.concatenate(three_parts(q_ref[...]), axis=0)
    for j in range(RING):
        if j % (RING // 2) == 0:
            for c in fetch[1 + j // 2 : 3 + j // 2]:
                c.wait()
        cols = pl.ds(j * width, width)
        term = jnp.dot(parts, g_ref[:, cols], preferred_element_type=F32)
        term += jnp.dot(parts, e_ref[:, cols], preferred_element_type=F32)
        local[j] = term[:rank] + term[rank : 2 * rank] + term[2 * rank :]
    for c in fetch[5:]:
        c.wait()
    for i in range(3):
        value = states[i]
        pre_a[z, i] = value[:, :128]
        pre_b[y, i] = jnp.concatenate([value[:, rows:], value[:, : 128 - rows]], axis=1)

    pl.semaphore_wait(barrier, 3 * (RING - 1))

    def state_copy(lane, step, way):
        axis, place, buf = (("z", z, pre_a), ("y", y, pre_b))[lane]
        block = down(place, step - 1) if way == 0 else up(place, step - 1)
        view = buf.at[block]
        if step == RING // 2:
            part = owned // 2
            view = buf.at[block, :, pl.ds(part * way, part)]
        return remote(state_sent.at[lane], state_came.at[lane, way * 4 + step - 1], axis, 1 if way == 0 else RING - 1, view, view)

    def state_landed(lane, step, way):
        axis, place, buf = (("z", z, pre_a), ("y", y, pre_b))[lane]
        block = down(place, step) if way == 0 else up(place, step)
        view = buf.at[block]
        if step == RING // 2:
            part = owned // 2
            view = buf.at[block, :, pl.ds(part * way, part)]
        return remote(state_sent.at[lane], state_came.at[lane, way * 4 + step - 1], axis, 1 if way == 0 else RING - 1, view, view)

    def state_step(step):
        for lane in range(2):
            for way in range(2):
                if step > 1:
                    state_landed(lane, step - 1, way).wait_recv()
                if step <= RING // 2:
                    state_copy(lane, step, way).start()

    step = half // CHUNKS
    chunks = range(CHUNKS)

    def near(c):
        return pl.ds(c * step, step)

    def far(c):
        return pl.ds(half + c * step, step)

    for c in chunks:
        for d in ORDER:
            send(0, 0, "z", d, local.at[up(z, d), near(c)], red_a.at[d - 1, near(c)], c)
            send(0, 1, "y", d, local.at[up(y, d), far(c)], red_b.at[d - 1, near(c)], c)
    state_step(1)
    others = pl.ds(0, RING - 1)
    for c in chunks:
        gathered(0, 0, red_a.at[:, near(c)], c)
        gathered(0, 1, red_b.at[:, near(c)], c)
        total_a = local[z, near(c)]
        total_b = local[y, far(c)]
        for i in range(RING - 1):
            total_a += red_a[i, near(c)]
            total_b += red_b[i, near(c)]
        sum_a[y, near(c)] = total_a
        sum_b[z, near(c)] = total_b
        for d in ORDER:
            send(1, 0, "y", d, sum_a.at[y, near(c)], sum_a.at[y, near(c)], c)
            send(1, 1, "z", d, sum_b.at[z, near(c)], sum_b.at[z, near(c)], c)
    state_step(2)
    for c in chunks:
        gathered(1, 0, sum_a.at[others, near(c)], c)
        gathered(1, 1, sum_b.at[others, near(c)], c)
        total_a = sum_a[0, near(c)]
        total_b = sum_b[0, near(c)]
        for i in range(1, RING):
            total_a += sum_a[i, near(c)]
            total_b += sum_b[i, near(c)]
        full[z, near(c)] = total_a
        full[y, far(c)] = total_b
        for d in ORDER:
            send(2, 0, "z", d, full.at[z, near(c)], full.at[z, near(c)], c)
            send(2, 1, "y", d, full.at[y, far(c)], full.at[y, far(c)], c)
    state_step(3)
    for c in chunks:
        gathered(2, 0, full.at[others, near(c)], c)
        gathered(2, 1, full.at[others, far(c)], c)

    whole = jnp.concatenate([full[j] for j in range(RING)], axis=1)
    parts = jnp.concatenate(three_parts(whole), axis=0)
    right = sum(
        lax.dot_general(parts, source[...], (((1,), (1,)), ((), ())), preferred_element_type=F32)
        for source in (g_ref, e_ref)
    )
    right = right[:rank] + right[rank : 2 * rank] + right[2 * rank :]
    rest = jnp.concatenate([right[:half, 128:192], right[half:, 128:192]], axis=1)
    fold_a[z, 0:16] = right[:half, :128]
    fold_a[z, 16:24] = rest[:8]
    fold_b[y, 0:16] = right[half:, :128]
    fold_b[y, 16:24] = rest[8:]
    for d in ORDER:
        send(3, 0, "z", d, fold_a.at[z], fold_a.at[z])
        send(3, 1, "y", d, fold_b.at[y], fold_b.at[y])
    state_step(4)

    gram = jnp.zeros((rank, rank), F32)
    for j in range(RING):
        gram += dot_nt(full[j], full[j])
    state = eliminate(widen(gram), 0, rank // 2)

    gathered(3, 0, fold_a.at[others])
    gathered(3, 1, fold_b.at[others])
    total_a = fold_a[0]
    total_b = fold_b[0]
    for i in range(1, RING):
        total_a += fold_a[i]
        total_b += fold_b[i]
    next_a[y] = total_a
    next_b[z] = total_b
    for d in ORDER:
        send(4, 0, "y", d, next_a.at[y], next_a.at[y])
        send(4, 1, "z", d, next_b.at[z], next_b.at[z])

    wide, pivots = eliminate(state, rank // 2, rank)
    inverse = (wide * lax.rsqrt(pivots))[:, rank : 2 * rank]
    from_col = lax.broadcasted_iota(jnp.int32, (width, width), 0)
    to_col = lax.broadcasted_iota(jnp.int32, (width, width), 1)
    picked = jnp.zeros((3 * rank, width), F32)
    for i in range(RING):
        chosen = jnp.where(
            (from_col - owned * z == to_col - owned * i) & (to_col >= owned * i) & (to_col < owned * (i + 1)),
            1.0, 0.0,
        ).astype(BF16)
        parts = jnp.concatenate(three_parts(full[i]), axis=0)
        picked += jnp.dot(parts, chosen, preferred_element_type=F32)
    picked = picked[:rank] + picked[rank : 2 * rank] + picked[2 * rank :]

    gathered(4, 0, next_a.at[others])
    gathered(4, 1, next_b.at[others])
    total_a = next_a[0]
    total_b = next_b[0]
    for i in range(1, RING):
        total_a += next_a[i]
        total_b += next_b[i]
    rest = jnp.concatenate([total_a[16:24], total_b[16:24]], axis=0)
    top = jnp.concatenate([total_a[0:16], total_b[0:16]], axis=0)
    rest = jnp.concatenate([rest[:, :64], rest[:, 64:]], axis=0)
    right = jnp.concatenate([top, rest], axis=1)
    right = dot_nn(inverse, right) * (1.0 / replicas)
    squares = jnp.sum(right * right, keepdims=True)
    norms[section] = jnp.broadcast_to(squares, (8, 128))
    for d in ORDER:
        send(5, 0, "s", d, norms.at[section], norms.at[section])
    right_ref[...] = right
    state_step(5)

    coef = dot_tn(inverse, right)
    grad_a[...] = dot_tn(full[y], coef[:, :128])
    grad_b[...] = dot_tn(picked, jnp.concatenate([coef[:, rows:], coef[:, : 128 - rows]], axis=1))
    high, low, _ = three_parts(coef)
    left = jnp.concatenate([high, high, low], axis=0)
    for j in range(RING):
        cols = pl.ds(j * width, width)
        high, low, _ = three_parts(full[j])
        approx = lax.dot_general(
            left, jnp.concatenate([high, low, high], axis=0), (((0,), (0,)), ((), ())),
            preferred_element_type=F32,
        )
        combined = g_ref[:, cols].astype(F32) + e_ref[:, cols].astype(F32)
        err_ref[:, cols] = (combined - approx).astype(BF16)

    gathered(5, 0, norms.at[others])
    squares = norms[0]
    for i in range(1, RING):
        squares += norms[i]
    clip = jnp.minimum(1.0, clip_limit / jnp.sqrt(squares))[0:1, 0:1]

    def update(grad, first, second, master):
        scaled = clip * grad
        new_first = beta_one * first + (1.0 - beta_one) * scaled
        new_second = beta_two * second + (1.0 - beta_two) * scaled * scaled
        adam_step = (
            new_first
            / (1.0 - beta_one**STEP)
            / (jnp.sqrt(new_second / (1.0 - beta_two**STEP)) + adam_epsilon)
        )
        return master - learn_rate * adam_step, new_first, new_second

    def group_update(grad, buf):
        first, second, master = (buf[:, i].reshape(width, 128) for i in range(3))
        return update(grad, first, second, master)[0]

    mine = pl.ds(pl.multiple_of(y * width, 128), width)
    out_ref[0:rows, mine] = group_update(grad_a[...], pre_a).astype(BF16).T[0:rows]

    if PIECES == 2:
        hops = (
            (2, 0, 0, 1), (-2, 0, 0, 1), (2, 0, 1, 1), (-2, 0, 1, 1),
            (1, 0, 0, 1), (-1, 0, 0, 1), (1, 0, 1, 1), (-1, 0, 1, 1),
            (2, -2, 0, 1), (1, -2, 0, 1), (1, -2, 1, 1), (-1, 2, 0, 1), (-1, 2, 1, 1), (-2, 2, 1, 1),
        )
        first, relay = 8, ((0, (8, 9)), (1, (11,)), (2, (10,)), (3, (13, 12)))
    else:
        hops = (
            (2, 0, 0, 2), (-2, 0, 0, 2), (1, 0, 0, 2), (-1, 0, 0, 2),
            (2, -2, 0, 1), (1, -2, 0, 2), (-2, 2, 1, 1), (-1, 2, 0, 2),
        )
        first, relay = 4, ((0, (4, 5)), (1, (6, 7)))

    def weight_copy(lane, sem, offset):
        axis, place = (("y", y), ("z", z))[lane]
        target, _, part, parts = hops[sem]
        block = up(place, offset % RING)
        if lane == 0:
            lanes = pl.ds(pl.multiple_of(block * width, 128), width)
            view = out_ref.at[pl.ds(part * (rows // 2), parts * (rows // 2)), lanes]
        else:
            view = tail_b.at[block, pl.ds(3 * part, 3 * parts)]
        came = weight_came.at[lane, min(sem, len(relay))]
        return remote(weight_sent.at[lane], came, axis, target % RING, view, view)

    def weight_view(lane, blocks):
        return out_ref.at[pl.ds(0, rows), pl.ds(0, blocks * width)] if lane == 0 else tail_b.at[pl.ds(0, blocks)]

    def weight_rest(lane):
        view = weight_view(lane, RING - 3)
        remote(weight_sent.at[lane], weight_came.at[lane, len(relay)], "z", 1, view, view).wait_recv()

    def weight_start(lane, sem):
        weight_copy(lane, sem, hops[sem][1]).start()

    def weight_landed(lane, sem):
        weight_copy(lane, sem, hops[sem][1] - hops[sem][0]).wait_recv()

    for sem in range(first):
        weight_start(0, sem)
    tail = group_update(grad_b[...], pre_b)
    lanes = lax.broadcasted_iota(jnp.int32, (owned, 128), 1)
    for i in range(6):
        other = tail[(6 + i % 2) * owned : (7 + i % 2) * owned]
        shift = rows - 32 * (i // 2)
        other = jnp.concatenate([other[:, 128 - shift :], other[:, : 128 - shift]], axis=1)
        tail_b[z, i] = jnp.where(lanes < rows, tail[i * owned : (i + 1) * owned], other).astype(BF16)
    for sem in range(first):
        weight_start(1, sem)

    own_a = grad_a[pl.ds(pl.multiple_of(z * owned, 8), owned)]
    own_b = grad_b[pl.ds(pl.multiple_of(y * owned, 8), owned)]
    grad = jnp.concatenate([own_a[:, :rows], own_b[:, :rows]], axis=1)
    new_master, new_first, new_second = update(grad, states[0], states[1], states[2])
    new_master_ref[...] = new_master
    new_first_ref[...] = new_first
    new_second_ref[...] = new_second

    for sem, onward in relay:
        for lane in (0, 1):
            weight_landed(lane, sem)
            for k in onward:
                weight_start(lane, k)
    weight_rest(1)
    for i in range(6):
        block = tail_b[:, i].reshape(width, 128).T
        out_ref[rows:, i * width : (i + 1) * width] = block[:rows]
        first_row = rows + 32 * (i // 2)
        first_col = (6 + i % 2) * width
        out_ref[first_row : first_row + 32, first_col : first_col + width] = block[rows:]
    weight_rest(0)
    for c in exchanges:
        c.wait_send()
    for lane in range(2):
        view = (pre_a, pre_b)[lane].at[others]
        remote(state_sent.at[lane], state_came.at[lane, 0], "z", 1, view, view).wait_send()
        view = weight_view(lane, RING - 1)
        remote(weight_sent.at[lane], weight_came.at[lane, 0], "z", 1, view, view).wait_send()


def finish_kernel(*refs):
    sources, targets, sems = refs[:6], refs[6:12], refs[12]
    copies = [pltpu.make_async_copy(s, t, sems.at[i]) for i, (s, t) in enumerate(zip(sources, targets))]
    for c in copies:
        c.start()
    for c in copies:
        c.wait()


def per_device(gradients, error_buffers, initial_q, master, first_moment, second_moment):
    rows, cols = gradients.shape[2:]
    rank = initial_q.shape[2]
    owned = master.shape[2]
    half = rank // 2
    width = cols // RING
    vmem = pl.BlockSpec(memory_space=pltpu.VMEM)
    hbm = pl.BlockSpec(memory_space=pltpu.HBM)
    shapes = (
        jax.ShapeDtypeStruct((rows, cols), BF16),
        jax.ShapeDtypeStruct((rank, rows), F32),
        jax.ShapeDtypeStruct((owned, rows), F32),
        jax.ShapeDtypeStruct((owned, rows), F32),
        jax.ShapeDtypeStruct((owned, rows), F32),
        jax.ShapeDtypeStruct((rows, cols), BF16),
    )
    operands = (gradients[0, 0], error_buffers[0, 0], initial_q[0].T)
    operands += (master[0].T, first_moment[0].T, second_moment[0].T)
    outs = pl.pallas_call(
        step_kernel,
        name="relay_step",
        out_shape=tuple(pltpu.VMEM(x.shape, x.dtype) for x in shapes),
        in_specs=[hbm] * 6,
        out_specs=(vmem,) * 6,
        scratch_shapes=[
            pltpu.VMEM((rows, cols), BF16),
            pltpu.VMEM((rows, cols), BF16),
            pltpu.VMEM((rank, rows), F32),
            pltpu.VMEM((3, owned, rows), F32),
            pltpu.VMEM((RING, rank, width), F32),
            pltpu.VMEM((RING - 1, half, width), F32),
            pltpu.VMEM((RING - 1, half, width), F32),
            pltpu.VMEM((RING, half, width), F32),
            pltpu.VMEM((RING, half, width), F32),
            pltpu.VMEM((RING, rank, width), F32),
            pltpu.VMEM((RING, 24, 128), F32),
            pltpu.VMEM((RING, 24, 128), F32),
            pltpu.VMEM((RING, 24, 128), F32),
            pltpu.VMEM((RING, 24, 128), F32),
            pltpu.VMEM((RING, 8, 128), F32),
            pltpu.VMEM((RING, 3, owned, 128), F32),
            pltpu.VMEM((RING, 3, owned, 128), F32),
            pltpu.VMEM((width, 128), F32),
            pltpu.VMEM((width, 128), F32),
            pltpu.VMEM((RING, 6, owned, 128), BF16),
            pltpu.SemaphoreType.DMA((8,)),
            pltpu.SemaphoreType.DMA((6 * CHUNKS + 5,)),
            pltpu.SemaphoreType.DMA((6 * CHUNKS + 5,)),
            pltpu.SemaphoreType.DMA((2,)),
            pltpu.SemaphoreType.DMA((2, 8)),
            pltpu.SemaphoreType.DMA((2,)),
            pltpu.SemaphoreType.DMA((2, 2 * PIECES + 1)),
        ],
        compiler_params=pltpu.CompilerParams(
            collective_id=0, has_side_effects=True, vmem_limit_bytes=40 << 20
        ),
    )(*(pltpu.with_memory_space_constraint(x, pltpu.HBM) for x in operands))
    outs = pl.pallas_call(
        finish_kernel,
        name="finish",
        out_shape=shapes,
        in_specs=[vmem] * 6,
        out_specs=(hbm,) * 6,
        scratch_shapes=[pltpu.SemaphoreType.DMA((6,))],
    )(*(pltpu.with_memory_space_constraint(x, pltpu.VMEM) for x in outs))
    new_errors, right, new_master, new_first, new_second, gathered = outs
    return (
        new_errors[None, None],
        right.T[None],
        new_master.T[None],
        new_first.T[None],
        new_second.T[None],
        gathered[None],
    )


def solution(mesh):
    placed = (
        P("section", "dp", None, None),
        P("section", "dp", None, None),
        P("section", None, None),
        P("section", None, "dp"),
        P("section", None, "dp"),
        P("section", None, "dp"),
    )
    return jax.shard_map(
        per_device,
        mesh=mesh,
        in_specs=placed,
        out_specs=(
            P("section", "dp", None, None),
            P("section", None, None),
            P("section", None, "dp"),
            P("section", None, "dp"),
            P("section", None, "dp"),
            P("section", None, None),
        ),
        check_vma=False,
    )
```

```python
import functools

import jax
import jax.numpy as jnp
from jax import lax
from jax.experimental import pallas as pl
from jax.experimental.pallas import tpu as pltpu
from jax.sharding import PartitionSpec as P

STEP = 10


beta_one = 0.9
beta_two = 0.999
adam_epsilon = 1e-08
learn_rate = 0.02
clip_limit = 16.0

RING = 8
CHUNKS = 2
PIECES = 2
ORDER = (4, 3, 5, 2, 6, 1, 7)
MESH = pl.DeviceIdType.MESH
HIGH = lax.Precision.HIGHEST
F32 = jnp.float32
BF16 = jnp.bfloat16


def dot_nn(a, b):
    return lax.dot_general(a, b, (((1,), (0,)), ((), ())), precision=HIGH, preferred_element_type=F32)


def dot_tn(a, b):
    return lax.dot_general(a, b, (((0,), (0,)), ((), ())), precision=HIGH, preferred_element_type=F32)


def dot_nt(a, b):
    return lax.dot_general(a, b, (((1,), (1,)), ((), ())), precision=HIGH, preferred_element_type=F32)


def three_parts(value):
    high = value.astype(BF16)
    rest = value - high.astype(F32)
    middle = rest.astype(BF16)
    low = (rest - middle.astype(F32)).astype(BF16)
    return high, middle, low


def widen(gram):
    rank = gram.shape[0]
    rows = lax.broadcasted_iota(jnp.int32, (rank, 128), 0)
    lanes = lax.broadcasted_iota(jnp.int32, (rank, 128), 1)
    identity = jnp.where(lanes == rows + rank, 1.0, 0.0).astype(F32)
    wide = jnp.concatenate([gram, jnp.zeros((rank, 128 - rank), F32)], axis=1) + identity
    return wide, jnp.ones((rank, 128), F32)


def eliminate(state, first, last):
    wide, pivots = state
    rank = wide.shape[0]
    rows = lax.broadcasted_iota(jnp.int32, (rank, 128), 0)
    for k in range(first, last):
        column = jnp.broadcast_to(wide[:, k : k + 1], (rank, 128))
        pivot = jnp.broadcast_to(column[k : k + 1, :], (rank, 128))
        row = jnp.broadcast_to(wide[k : k + 1, :], (rank, 128))
        pivots = jnp.where(rows == k, pivot, pivots)
        factor = jnp.where(rows > k, column / pivot, 0.0)
        wide = wide - factor * row
    return wide, pivots


def step_kernel(
    g_hbm, e_hbm, q_hbm, master_hbm, first_hbm, second_hbm,
    err_ref, right_ref, new_master_ref, new_first_ref, new_second_ref, out_ref,
    g_ref, e_ref, q_ref, states, local, red, sums, full, folds, nexts,
    norms, pre, grad_a, grad_b, tail_b, tally, loads, sent, landed, state_came, weight_came,
):
    section = lax.axis_index("section")
    dp = lax.axis_index("dp")
    y = lax.div(dp, RING)
    z = lax.rem(dp, RING)
    replicas = RING * RING
    rank = q_ref.shape[0]
    half = rank // 2
    width = g_ref.shape[1] // RING
    owned = master_hbm.shape[0]
    rows = g_ref.shape[0] // 2

    def up(i, d):
        return lax.rem(i + d, RING)

    def down(i, d):
        return lax.rem(i + RING - d, RING)

    def peer(axis, d):
        if axis == "z":
            return (section, y * RING + up(z, d))
        if axis == "y":
            return (section, up(y, d) * RING + z)
        return (up(section, d), dp)

    def remote(recv_sem, axis, d, src, dst):
        return pltpu.make_async_remote_copy(
            src_ref=src, dst_ref=dst, send_sem=sent.at[0], recv_sem=recv_sem,
            device_id=peer(axis, d), device_id_type=MESH,
        )

    def send(phase, axis, d, src, dst, chunk=0):
        remote(landed.at[phase, chunk], axis, d, src, dst).start()

    def gathered(phase, view, chunk=0):
        remote(landed.at[phase, chunk], "z", 1, view, view).wait_recv()

    middle = (RING // 2) * width
    fetch = [(0, q_hbm, q_ref)]
    for i in range(2):
        cols = pl.ds(i * middle, middle)
        fetch += [(1 + i, g_hbm.at[:, cols], g_ref.at[:, cols]), (1 + i, e_hbm.at[:, cols], e_ref.at[:, cols])]
    fetch += [(3, x, states.at[i]) for i, x in enumerate((first_hbm, second_hbm, master_hbm))]
    for i, x, v in fetch:
        pltpu.make_async_copy(x, v, loads.at[i]).start()

    def loaded(i, view):
        pltpu.make_async_copy(view, view, loads.at[i]).wait()

    barrier = pltpu.get_barrier_semaphore()
    for axis in ("z", "y", "s"):
        for d in range(1, RING):
            pl.semaphore_signal(barrier, 1, device_id=peer(axis, d), device_id_type=MESH)

    loaded(0, q_ref)
    parts = jnp.concatenate(three_parts(q_ref[...]), axis=0)
    for j in range(RING):
        if j % (RING // 2) == 0:
            loaded(1 + j // (RING // 2), g_ref)
        cols = pl.ds(j * width, width)
        term = jnp.dot(parts, g_ref[:, cols], preferred_element_type=F32)
        term += jnp.dot(parts, e_ref[:, cols], preferred_element_type=F32)
        local[j] = term[:rank] + term[rank : 2 * rank] + term[2 * rank :]
    loaded(3, states)
    for i in range(3):
        value = states[i]
        pre[0, z, i] = value[:, :128]
        pre[1, y, i] = jnp.concatenate([value[:, rows:], value[:, : 128 - rows]], axis=1)

    pl.semaphore_wait(barrier, 3 * (RING - 1))

    def state_step(step):
        if step > 1:
            view = pre.at[0, pl.ds(0, 4 if step <= RING // 2 else 2)]
            remote(state_came.at[step - 2], "z", 1, view, view).wait_recv()
        if step > RING // 2:
            return
        for lane, (axis, place) in enumerate((("z", z), ("y", y))):
            for way, block in enumerate((down(place, step - 1), up(place, step - 1))):
                view = pre.at[lane, block]
                if step == RING // 2:
                    view = pre.at[lane, block, :, pl.ds(owned // 2 * way, owned // 2)]
                remote(state_came.at[step - 1], axis, (1, RING - 1)[way], view, view).start()

    step = half // CHUNKS
    chunks = range(CHUNKS)

    def near(c):
        return pl.ds(c * step, step)

    def far(c):
        return pl.ds(half + c * step, step)

    for c in chunks:
        for d in ORDER:
            send(0, "z", d, local.at[up(z, d), near(c)], red.at[0, d - 1, near(c)], c)
            send(0, "y", d, local.at[up(y, d), far(c)], red.at[1, d - 1, near(c)], c)
    state_step(1)
    others = pl.ds(0, RING - 1)
    for c in chunks:
        gathered(0, red.at[:, :, near(c)], c)
        total_a = local[z, near(c)]
        total_b = local[y, far(c)]
        for i in range(RING - 1):
            total_a += red[0, i, near(c)]
            total_b += red[1, i, near(c)]
        sums[0, y, near(c)] = total_a
        sums[1, z, near(c)] = total_b
        for d in ORDER:
            send(1, "y", d, sums.at[0, y, near(c)], sums.at[0, y, near(c)], c)
            send(1, "z", d, sums.at[1, z, near(c)], sums.at[1, z, near(c)], c)
    state_step(2)
    for c in chunks:
        gathered(1, sums.at[:, others, near(c)], c)
        total_a = sums[0, 0, near(c)]
        total_b = sums[1, 0, near(c)]
        for i in range(1, RING):
            total_a += sums[0, i, near(c)]
            total_b += sums[1, i, near(c)]
        full[z, near(c)] = total_a
        full[y, far(c)] = total_b
        for d in ORDER:
            send(2, "z", d, full.at[z, near(c)], full.at[z, near(c)], c)
            send(2, "y", d, full.at[y, far(c)], full.at[y, far(c)], c)
    state_step(3)
    for c in chunks:
        gathered(2, full.at[others, pl.ds(0, 2 * step)], c)

    whole = jnp.concatenate([full[j] for j in range(RING)], axis=1)
    parts = jnp.concatenate(three_parts(whole), axis=0)
    right = sum(
        lax.dot_general(parts, source[...], (((1,), (1,)), ((), ())), preferred_element_type=F32)
        for source in (g_ref, e_ref)
    )
    right = right[:rank] + right[rank : 2 * rank] + right[2 * rank :]
    rest = jnp.concatenate([right[:half, 128:192], right[half:, 128:192]], axis=1)
    folds[0, z, 0:16] = right[:half, :128]
    folds[0, z, 16:24] = rest[:8]
    folds[1, y, 0:16] = right[half:, :128]
    folds[1, y, 16:24] = rest[8:]
    for d in ORDER:
        send(3, "z", d, folds.at[0, z], folds.at[0, z])
        send(3, "y", d, folds.at[1, y], folds.at[1, y])
    state_step(4)

    gram = jnp.zeros((rank, rank), F32)
    for j in range(RING):
        gram += dot_nt(full[j], full[j])
    state = eliminate(widen(gram), 0, rank // 2)

    gathered(3, folds.at[:, others])
    total_a = folds[0, 0]
    total_b = folds[1, 0]
    for i in range(1, RING):
        total_a += folds[0, i]
        total_b += folds[1, i]
    nexts[0, y] = total_a
    nexts[1, z] = total_b
    for d in ORDER:
        send(4, "y", d, nexts.at[0, y], nexts.at[0, y])
        send(4, "z", d, nexts.at[1, z], nexts.at[1, z])

    wide, pivots = eliminate(state, rank // 2, rank)
    inverse = (wide * lax.rsqrt(pivots))[:, rank : 2 * rank]
    from_col = lax.broadcasted_iota(jnp.int32, (width, width), 0)
    to_col = lax.broadcasted_iota(jnp.int32, (width, width), 1)
    picked = jnp.zeros((3 * rank, width), F32)
    for i in range(RING):
        chosen = jnp.where(
            (from_col - owned * z == to_col - owned * i) & (to_col >= owned * i) & (to_col < owned * (i + 1)),
            1.0, 0.0,
        ).astype(BF16)
        parts = jnp.concatenate(three_parts(full[i]), axis=0)
        picked += jnp.dot(parts, chosen, preferred_element_type=F32)
    picked = picked[:rank] + picked[rank : 2 * rank] + picked[2 * rank :]

    gathered(4, nexts.at[:, others])
    total_a = nexts[0, 0]
    total_b = nexts[1, 0]
    for i in range(1, RING):
        total_a += nexts[0, i]
        total_b += nexts[1, i]
    rest = jnp.concatenate([total_a[16:24], total_b[16:24]], axis=0)
    top = jnp.concatenate([total_a[0:16], total_b[0:16]], axis=0)
    rest = jnp.concatenate([rest[:, :64], rest[:, 64:]], axis=0)
    right = jnp.concatenate([top, rest], axis=1)
    right = dot_nn(inverse, right) * (1.0 / replicas)
    squares = jnp.sum(right * right, keepdims=True)
    norms[section] = jnp.broadcast_to(squares, (8, 128))
    for d in ORDER:
        send(5, "s", d, norms.at[section], norms.at[section])
    right_ref[...] = right
    state_step(5)

    coef = dot_tn(inverse, right)
    grad_a[...] = dot_tn(full[y], coef[:, :128])
    grad_b[...] = dot_tn(picked, jnp.concatenate([coef[:, rows:], coef[:, : 128 - rows]], axis=1))
    high, low, _ = three_parts(coef)
    left = jnp.concatenate([high, high, low], axis=0)
    for j in range(RING):
        cols = pl.ds(j * width, width)
        high, low, _ = three_parts(full[j])
        approx = lax.dot_general(
            left, jnp.concatenate([high, low, high], axis=0), (((0,), (0,)), ((), ())),
            preferred_element_type=F32,
        )
        combined = g_ref[:, cols].astype(F32) + e_ref[:, cols].astype(F32)
        err_ref[:, cols] = (combined - approx).astype(BF16)

    gathered(5, norms.at[others])
    squares = norms[0]
    for i in range(1, RING):
        squares += norms[i]
    clip = jnp.minimum(1.0, clip_limit / jnp.sqrt(squares))[0:1, 0:1]

    def update(grad, first, second, master):
        scaled = clip * grad
        new_first = beta_one * first + (1.0 - beta_one) * scaled
        new_second = beta_two * second + (1.0 - beta_two) * scaled * scaled
        adam_step = (
            new_first
            / (1.0 - beta_one**STEP)
            / (jnp.sqrt(new_second / (1.0 - beta_two**STEP)) + adam_epsilon)
        )
        return master - learn_rate * adam_step, new_first, new_second

    def group_update(grad, lane):
        first, second, master = (pre[lane, :, i].reshape(width, 128) for i in range(3))
        return update(grad, first, second, master)[0]

    mine = pl.ds(pl.multiple_of(y * width, 128), width)
    out_ref[0:rows, mine] = group_update(grad_a[...], 0).astype(BF16).T[0:rows]

    if PIECES == 2:
        hops = (
            (2, 0, 0, 1), (-2, 0, 0, 1), (2, 0, 1, 1), (-2, 0, 1, 1),
            (1, 0, 0, 1), (-1, 0, 0, 1), (1, 0, 1, 1), (-1, 0, 1, 1),
            (2, -2, 0, 1), (1, -2, 0, 1), (1, -2, 1, 1), (-1, 2, 0, 1), (-1, 2, 1, 1), (-2, 2, 1, 1),
        )
        first, relay = 8, ((0, (8, 9)), (1, (11,)), (2, (10,)), (3, (13, 12)))
    else:
        hops = (
            (2, 0, 0, 2), (-2, 0, 0, 2), (1, 0, 0, 2), (-1, 0, 0, 2),
            (2, -2, 0, 1), (1, -2, 0, 2), (-2, 2, 1, 1), (-1, 2, 0, 2),
        )
        first, relay = 4, ((0, (4, 5)), (1, (6, 7)))

    def weight_copy(lane, sem, offset):
        axis, place = (("y", y), ("z", z))[lane]
        target, _, part, parts = hops[sem]
        block = up(place, offset % RING)
        if lane == 0:
            lanes = pl.ds(pl.multiple_of(block * width, 128), width)
            view = out_ref.at[pl.ds(part * (rows // 2), parts * (rows // 2)), lanes]
        else:
            view = tail_b.at[block, pl.ds(3 * part, 3 * parts)]
        came = weight_came.at[lane, min(sem, len(relay))]
        return remote(came, axis, target % RING, view, view)

    def weight_view(lane, blocks):
        return out_ref.at[pl.ds(0, rows), pl.ds(0, blocks * width)] if lane == 0 else tail_b.at[pl.ds(0, blocks)]

    def weight_rest(lane):
        view = weight_view(lane, RING - 3)
        remote(weight_came.at[lane, len(relay)], "z", 1, view, view).wait_recv()

    def weight_start(lane, sem):
        weight_copy(lane, sem, hops[sem][1]).start()

    def weight_landed(lane, sem):
        weight_copy(lane, sem, hops[sem][1] - hops[sem][0]).wait_recv()

    for sem in range(first):
        weight_start(0, sem)
    tail = group_update(grad_b[...], 1)
    lanes = lax.broadcasted_iota(jnp.int32, (owned, 128), 1)
    for i in range(6):
        other = tail[(6 + i % 2) * owned : (7 + i % 2) * owned]
        shift = rows - 32 * (i // 2)
        other = jnp.concatenate([other[:, 128 - shift :], other[:, : 128 - shift]], axis=1)
        tail_b[z, i] = jnp.where(lanes < rows, tail[i * owned : (i + 1) * owned], other).astype(BF16)
    for sem in range(first):
        weight_start(1, sem)

    own_a = grad_a[pl.ds(pl.multiple_of(z * owned, 8), owned)]
    own_b = grad_b[pl.ds(pl.multiple_of(y * owned, 8), owned)]
    grad = jnp.concatenate([own_a[:, :rows], own_b[:, :rows]], axis=1)
    new_master, new_first, new_second = update(grad, states[0], states[1], states[2])
    new_master_ref[...] = new_master
    new_first_ref[...] = new_first
    new_second_ref[...] = new_second

    for pair in (relay[:2], relay[2:]):
        for lane in (0, 1):
            for sem, onward in pair:
                weight_landed(lane, sem)
                for k in onward:
                    weight_start(lane, k)
    weight_rest(1)
    for i in range(6):
        block = tail_b[:, i].reshape(width, 128).T
        out_ref[rows:, i * width : (i + 1) * width] = block[:rows]
        first_row = rows + 32 * (i // 2)
        first_col = (6 + i % 2) * width
        out_ref[first_row : first_row + 32, first_col : first_col + width] = block[rows:]
    weight_rest(0)
    remote(weight_came.at[0, 0], "z", 1, tally, tally).wait_send()


def finish_kernel(*refs):
    sources, targets, sems = refs[:6], refs[6:12], refs[12]
    copies = [pltpu.make_async_copy(s, t, sems.at[i]) for i, (s, t) in enumerate(zip(sources, targets))]
    for c in copies:
        c.start()
    for c in copies:
        c.wait()


def per_device(gradients, error_buffers, initial_q, master, first_moment, second_moment):
    rows, cols = gradients.shape[2:]
    rank = initial_q.shape[2]
    owned = master.shape[2]
    half = rank // 2
    width = cols // RING
    blocks = 2 * (RING - 1)
    exchanged = 3 * half * width + 2 * 24 * 128 + 4 * 128 + 3 * owned * 128 + rows // 2 * width // 2
    tally_rows = blocks * exchanged // 128
    vmem = pl.BlockSpec(memory_space=pltpu.VMEM)
    hbm = pl.BlockSpec(memory_space=pltpu.HBM)
    shapes = (
        jax.ShapeDtypeStruct((rows, cols), BF16),
        jax.ShapeDtypeStruct((rank, rows), F32),
        jax.ShapeDtypeStruct((owned, rows), F32),
        jax.ShapeDtypeStruct((owned, rows), F32),
        jax.ShapeDtypeStruct((owned, rows), F32),
        jax.ShapeDtypeStruct((rows, cols), BF16),
    )
    operands = (gradients[0, 0], error_buffers[0, 0], initial_q[0].T)
    operands += (master[0].T, first_moment[0].T, second_moment[0].T)
    outs = pl.pallas_call(
        step_kernel,
        name="relay_step",
        out_shape=tuple(pltpu.VMEM(x.shape, x.dtype) for x in shapes),
        in_specs=[hbm] * 6,
        out_specs=(vmem,) * 6,
        scratch_shapes=[
            pltpu.VMEM((rows, cols), BF16),
            pltpu.VMEM((rows, cols), BF16),
            pltpu.VMEM((rank, rows), F32),
            pltpu.VMEM((3, owned, rows), F32),
            pltpu.VMEM((RING, rank, width), F32),
            pltpu.VMEM((2, RING - 1, half, width), F32),
            pltpu.VMEM((2, RING, half, width), F32),
            pltpu.VMEM((RING, rank, width), F32),
            pltpu.VMEM((2, RING, 24, 128), F32),
            pltpu.VMEM((2, RING, 24, 128), F32),
            pltpu.VMEM((RING, 8, 128), F32),
            pltpu.VMEM((2, RING, 3, owned, 128), F32),
            pltpu.VMEM((width, 128), F32),
            pltpu.VMEM((width, 128), F32),
            pltpu.VMEM((RING, 6, owned, 128), BF16),
            pltpu.VMEM((tally_rows, 128), F32),
            pltpu.SemaphoreType.DMA((4,)),
            pltpu.SemaphoreType.DMA((1,)),
            pltpu.SemaphoreType.DMA((6, CHUNKS)),
            pltpu.SemaphoreType.DMA((4,)),
            pltpu.SemaphoreType.DMA((2, 2 * PIECES + 1)),
        ],
        compiler_params=pltpu.CompilerParams(
            collective_id=0, has_side_effects=True, vmem_limit_bytes=40 << 20
        ),
    )(*(pltpu.with_memory_space_constraint(x, pltpu.HBM) for x in operands))
    outs = pl.pallas_call(
        finish_kernel,
        name="finish",
        out_shape=shapes,
        in_specs=[vmem] * 6,
        out_specs=(hbm,) * 6,
        scratch_shapes=[pltpu.SemaphoreType.DMA((6,))],
    )(*(pltpu.with_memory_space_constraint(x, pltpu.VMEM) for x in outs))
    new_errors, right, new_master, new_first, new_second, gathered = outs
    return (
        new_errors[None, None],
        right.T[None],
        new_master.T[None],
        new_first.T[None],
        new_second.T[None],
        gathered[None],
    )


def solution(mesh):
    placed = (
        P("section", "dp", None, None),
        P("section", "dp", None, None),
        P("section", None, None),
        P("section", None, "dp"),
        P("section", None, "dp"),
        P("section", None, "dp"),
    )
    return jax.shard_map(
        per_device,
        mesh=mesh,
        in_specs=placed,
        out_specs=(
            P("section", "dp", None, None),
            P("section", None, None),
            P("section", None, "dp"),
            P("section", None, "dp"),
            P("section", None, "dp"),
            P("section", None, None),
        ),
        check_vma=False,
    )
```

```python
import functools

import jax
import jax.numpy as jnp
from jax import lax
from jax.experimental import pallas as pl
from jax.experimental.pallas import tpu as pltpu
from jax.sharding import PartitionSpec as P

STEP = 10


beta_one = 0.9
beta_two = 0.999
adam_epsilon = 1e-08
learn_rate = 0.02
clip_limit = 16.0

RING = 8
ROW_CHUNKS = 2
LANE_CHUNKS = 1
CHUNKS = ROW_CHUNKS * LANE_CHUNKS
PIECES = 2
ORDER = (4, 3, 5, 2, 6, 1, 7)
MESH = pl.DeviceIdType.MESH
HIGH = lax.Precision.HIGHEST
F32 = jnp.float32
BF16 = jnp.bfloat16


def dot_nn(a, b):
    return lax.dot_general(a, b, (((1,), (0,)), ((), ())), precision=HIGH, preferred_element_type=F32)


def dot_tn(a, b):
    return lax.dot_general(a, b, (((0,), (0,)), ((), ())), precision=HIGH, preferred_element_type=F32)


def dot_nt(a, b):
    return lax.dot_general(a, b, (((1,), (1,)), ((), ())), precision=HIGH, preferred_element_type=F32)


def three_parts(value):
    high = value.astype(BF16)
    rest = value - high.astype(F32)
    middle = rest.astype(BF16)
    low = (rest - middle.astype(F32)).astype(BF16)
    return high, middle, low


def widen(gram):
    rank = gram.shape[0]
    rows = lax.broadcasted_iota(jnp.int32, (rank, 128), 0)
    lanes = lax.broadcasted_iota(jnp.int32, (rank, 128), 1)
    identity = jnp.where(lanes == rows + rank, 1.0, 0.0).astype(F32)
    wide = jnp.concatenate([gram, jnp.zeros((rank, 128 - rank), F32)], axis=1) + identity
    return wide, jnp.ones((rank, 128), F32)


def eliminate(state, first, last):
    wide, pivots = state
    rank = wide.shape[0]
    rows = lax.broadcasted_iota(jnp.int32, (rank, 128), 0)
    for k in range(first, last):
        column = jnp.broadcast_to(wide[:, k : k + 1], (rank, 128))
        pivot = jnp.broadcast_to(column[k : k + 1, :], (rank, 128))
        row = jnp.broadcast_to(wide[k : k + 1, :], (rank, 128))
        pivots = jnp.where(rows == k, pivot, pivots)
        factor = jnp.where(rows > k, column / pivot, 0.0)
        wide = wide - factor * row
    return wide, pivots


def step_kernel(
    g_hbm, e_hbm, q_hbm, master_hbm, first_hbm, second_hbm,
    err_ref, right_ref, new_master_ref, new_first_ref, new_second_ref, out_ref,
    g_ref, e_ref, q_ref, states, local, red, sums, full, folds, nexts,
    norms, pre, grad_a, grad_b, tail_b, tally, loads, sent, landed, state_came, weight_came,
):
    section = lax.axis_index("section")
    dp = lax.axis_index("dp")
    y = lax.div(dp, RING)
    z = lax.rem(dp, RING)
    replicas = RING * RING
    rank = q_ref.shape[0]
    half = rank // 2
    width = g_ref.shape[1] // RING
    owned = master_hbm.shape[0]
    rows = g_ref.shape[0] // 2

    def up(i, d):
        return lax.rem(i + d, RING)

    def down(i, d):
        return lax.rem(i + RING - d, RING)

    def peer(axis, d):
        if axis == "z":
            return (section, y * RING + up(z, d))
        if axis == "y":
            return (section, up(y, d) * RING + z)
        return (up(section, d), dp)

    def remote(recv_sem, axis, d, src, dst):
        return pltpu.make_async_remote_copy(
            src_ref=src, dst_ref=dst, send_sem=sent.at[0], recv_sem=recv_sem,
            device_id=peer(axis, d), device_id_type=MESH,
        )

    def send(phase, axis, d, src, dst, chunk=0):
        remote(landed.at[phase, chunk], axis, d, src, dst).start()

    def gathered(phase, view, chunk=0):
        remote(landed.at[phase, chunk], "z", 1, view, view).wait_recv()

    middle = (RING // 2) * width
    fetch = [(0, q_hbm, q_ref)]
    for i in range(2):
        cols = pl.ds(i * middle, middle)
        fetch += [(1 + i, g_hbm.at[:, cols], g_ref.at[:, cols]), (1 + i, e_hbm.at[:, cols], e_ref.at[:, cols])]
    fetch += [(3, x, states.at[i]) for i, x in enumerate((first_hbm, second_hbm, master_hbm))]
    for i, x, v in fetch:
        pltpu.make_async_copy(x, v, loads.at[i]).start()

    def loaded(i, view):
        pltpu.make_async_copy(view, view, loads.at[i]).wait()

    barrier = pltpu.get_barrier_semaphore()
    for axis in ("z", "y", "s"):
        for d in range(1, RING):
            pl.semaphore_signal(barrier, 1, device_id=peer(axis, d), device_id_type=MESH)

    loaded(0, q_ref)
    parts = jnp.concatenate(three_parts(q_ref[...]), axis=0)
    for j in range(RING):
        if j % (RING // 2) == 0:
            loaded(1 + j // (RING // 2), g_ref)
        cols = pl.ds(j * width, width)
        term = jnp.dot(parts, g_ref[:, cols], preferred_element_type=F32)
        term += jnp.dot(parts, e_ref[:, cols], preferred_element_type=F32)
        local[j] = term[:rank] + term[rank : 2 * rank] + term[2 * rank :]
    pl.semaphore_wait(barrier, 3 * (RING - 1))

    def state_step(step):
        if step > 1:
            view = pre.at[0, pl.ds(0, 4 if step <= RING // 2 else 2)]
            remote(state_came.at[step - 2], "z", 1, view, view).wait_recv()
        if step > RING // 2:
            return
        for lane, (axis, place) in enumerate((("z", z), ("y", y))):
            for way, block in enumerate((down(place, step - 1), up(place, step - 1))):
                view = pre.at[lane, block]
                if step == RING // 2:
                    view = pre.at[lane, block, :, pl.ds(owned // 2 * way, owned // 2)]
                remote(state_came.at[step - 1], axis, (1, RING - 1)[way], view, view).start()

    step = half // ROW_CHUNKS
    span = width // LANE_CHUNKS
    chunks = range(CHUNKS)

    def near(c):
        return pl.ds(c // LANE_CHUNKS * step, step), pl.ds(c % LANE_CHUNKS * span, span)

    def far(c):
        return pl.ds(half + c // LANE_CHUNKS * step, step), pl.ds(c % LANE_CHUNKS * span, span)

    for c in chunks:
        for d in ORDER:
            send(0, "z", d, local.at[up(z, d), *near(c)], red.at[0, d - 1, *near(c)], c)
            send(0, "y", d, local.at[up(y, d), *far(c)], red.at[1, d - 1, *near(c)], c)
    loaded(3, states)
    for i in range(3):
        value = states[i]
        pre[0, z, i] = value[:, :128]
        pre[1, y, i] = jnp.concatenate([value[:, rows:], value[:, : 128 - rows]], axis=1)
    state_step(1)
    others = pl.ds(0, RING - 1)
    for c in chunks:
        gathered(0, red.at[:, :, *near(c)], c)
        total_a = local[z, *near(c)]
        total_b = local[y, *far(c)]
        for i in range(RING - 1):
            total_a += red[0, i, *near(c)]
            total_b += red[1, i, *near(c)]
        sums[0, y, *near(c)] = total_a
        sums[1, z, *near(c)] = total_b
        for d in ORDER:
            send(1, "y", d, sums.at[0, y, *near(c)], sums.at[0, y, *near(c)], c)
            send(1, "z", d, sums.at[1, z, *near(c)], sums.at[1, z, *near(c)], c)
    state_step(2)
    for c in chunks:
        gathered(1, sums.at[:, others, *near(c)], c)
        total_a = sums[0, 0, *near(c)]
        total_b = sums[1, 0, *near(c)]
        for i in range(1, RING):
            total_a += sums[0, i, *near(c)]
            total_b += sums[1, i, *near(c)]
        full[z, *near(c)] = total_a
        full[y, *far(c)] = total_b
        for d in ORDER:
            send(2, "z", d, full.at[z, *near(c)], full.at[z, *near(c)], c)
            send(2, "y", d, full.at[y, *far(c)], full.at[y, *far(c)], c)
    state_step(3)
    for c in chunks:
        gathered(2, full.at[others, pl.ds(0, 2 * step), pl.ds(0, span)], c)

    whole = jnp.concatenate([full[j] for j in range(RING)], axis=1)
    parts = jnp.concatenate(three_parts(whole), axis=0)
    right = sum(
        lax.dot_general(parts, source[...], (((1,), (1,)), ((), ())), preferred_element_type=F32)
        for source in (g_ref, e_ref)
    )
    right = right[:rank] + right[rank : 2 * rank] + right[2 * rank :]
    rest = jnp.concatenate([right[:half, 128:192], right[half:, 128:192]], axis=1)
    folds[0, z, 0:16] = right[:half, :128]
    folds[0, z, 16:24] = rest[:8]
    folds[1, y, 0:16] = right[half:, :128]
    folds[1, y, 16:24] = rest[8:]
    for d in ORDER:
        send(3, "z", d, folds.at[0, z], folds.at[0, z])
        send(3, "y", d, folds.at[1, y], folds.at[1, y])
    state_step(4)

    gram = jnp.zeros((rank, rank), F32)
    for j in range(RING):
        gram += dot_nt(full[j], full[j])
    state = eliminate(widen(gram), 0, rank // 2)

    gathered(3, folds.at[:, others])
    total_a = folds[0, 0]
    total_b = folds[1, 0]
    for i in range(1, RING):
        total_a += folds[0, i]
        total_b += folds[1, i]
    nexts[0, y] = total_a
    nexts[1, z] = total_b
    for d in ORDER:
        send(4, "y", d, nexts.at[0, y], nexts.at[0, y])
        send(4, "z", d, nexts.at[1, z], nexts.at[1, z])

    wide, pivots = eliminate(state, rank // 2, rank)
    inverse = (wide * lax.rsqrt(pivots))[:, rank : 2 * rank]
    from_col = lax.broadcasted_iota(jnp.int32, (width, width), 0)
    to_col = lax.broadcasted_iota(jnp.int32, (width, width), 1)
    picked = jnp.zeros((3 * rank, width), F32)
    for i in range(RING):
        chosen = jnp.where(
            (from_col - owned * z == to_col - owned * i) & (to_col >= owned * i) & (to_col < owned * (i + 1)),
            1.0, 0.0,
        ).astype(BF16)
        parts = jnp.concatenate(three_parts(full[i]), axis=0)
        picked += jnp.dot(parts, chosen, preferred_element_type=F32)
    picked = picked[:rank] + picked[rank : 2 * rank] + picked[2 * rank :]

    gathered(4, nexts.at[:, others])
    total_a = nexts[0, 0]
    total_b = nexts[1, 0]
    for i in range(1, RING):
        total_a += nexts[0, i]
        total_b += nexts[1, i]
    rest = jnp.concatenate([total_a[16:24], total_b[16:24]], axis=0)
    top = jnp.concatenate([total_a[0:16], total_b[0:16]], axis=0)
    rest = jnp.concatenate([rest[:, :64], rest[:, 64:]], axis=0)
    right = jnp.concatenate([top, rest], axis=1)
    right = dot_nn(inverse, right) * (1.0 / replicas)
    squares = jnp.sum(right * right, keepdims=True)
    norms[section] = jnp.broadcast_to(squares, (8, 128))
    for d in ORDER:
        send(5, "s", d, norms.at[section], norms.at[section])
    right_ref[...] = right
    state_step(5)

    coef = dot_tn(inverse, right)
    grad_a[...] = dot_tn(full[y], coef[:, :128])
    grad_b[...] = dot_tn(picked, jnp.concatenate([coef[:, rows:], coef[:, : 128 - rows]], axis=1))
    high, low, _ = three_parts(coef)
    left = jnp.concatenate([high, high, low], axis=0)
    for j in range(RING):
        cols = pl.ds(j * width, width)
        high, low, _ = three_parts(full[j])
        approx = lax.dot_general(
            left, jnp.concatenate([high, low, high], axis=0), (((0,), (0,)), ((), ())),
            preferred_element_type=F32,
        )
        combined = g_ref[:, cols].astype(F32) + e_ref[:, cols].astype(F32)
        err_ref[:, cols] = (combined - approx).astype(BF16)

    gathered(5, norms.at[others])
    squares = norms[0]
    for i in range(1, RING):
        squares += norms[i]
    clip = jnp.minimum(1.0, clip_limit / jnp.sqrt(squares))[0:1, 0:1]

    def update(grad, first, second, master):
        scaled = clip * grad
        new_first = beta_one * first + (1.0 - beta_one) * scaled
        new_second = beta_two * second + (1.0 - beta_two) * scaled * scaled
        rate = learn_rate / (1.0 - beta_one**STEP)
        spread = jnp.sqrt(new_second * (1.0 / (1.0 - beta_two**STEP))) + adam_epsilon
        return master - rate * new_first / spread, new_first, new_second

    def group_update(grad, lane):
        first, second, master = (pre[lane, :, i].reshape(width, 128) for i in range(3))
        return update(grad, first, second, master)[0]

    mine = pl.ds(pl.multiple_of(y * width, 128), width)
    out_ref[0:rows, mine] = group_update(grad_a[...], 0).astype(BF16).T[0:rows]

    if PIECES == 2:
        hops = (
            (2, 0, 0, 1), (-2, 0, 0, 1), (2, 0, 1, 1), (-2, 0, 1, 1),
            (1, 0, 0, 1), (-1, 0, 0, 1), (1, 0, 1, 1), (-1, 0, 1, 1),
            (2, -2, 0, 1), (1, -2, 0, 1), (1, -2, 1, 1), (-1, 2, 0, 1), (-1, 2, 1, 1), (-2, 2, 1, 1),
        )
        first, relay = 8, ((0, (8, 9)), (1, (11,)), (2, (10,)), (3, (13, 12)))
    else:
        hops = (
            (2, 0, 0, 2), (-2, 0, 0, 2), (1, 0, 0, 2), (-1, 0, 0, 2),
            (2, -2, 0, 1), (1, -2, 0, 2), (-2, 2, 1, 1), (-1, 2, 0, 2),
        )
        first, relay = 4, ((0, (4, 5)), (1, (6, 7)))

    def weight_copy(lane, sem, offset):
        axis, place = (("y", y), ("z", z))[lane]
        target, _, part, parts = hops[sem]
        block = up(place, offset % RING)
        if lane == 0:
            lanes = pl.ds(pl.multiple_of(block * width, 128), width)
            view = out_ref.at[pl.ds(part * (rows // 2), parts * (rows // 2)), lanes]
        else:
            view = tail_b.at[block, pl.ds(3 * part, 3 * parts)]
        came = weight_came.at[lane, min(sem, len(relay))]
        return remote(came, axis, target % RING, view, view)

    def weight_view(lane, blocks):
        return out_ref.at[pl.ds(0, rows), pl.ds(0, blocks * width)] if lane == 0 else tail_b.at[pl.ds(0, blocks)]

    def weight_rest(lane):
        view = weight_view(lane, RING - 3)
        remote(weight_came.at[lane, len(relay)], "z", 1, view, view).wait_recv()

    def weight_start(lane, sem):
        weight_copy(lane, sem, hops[sem][1]).start()

    def weight_landed(lane, sem):
        weight_copy(lane, sem, hops[sem][1] - hops[sem][0]).wait_recv()

    for sem in range(first):
        weight_start(0, sem)
    tail = group_update(grad_b[...], 1)
    lanes = lax.broadcasted_iota(jnp.int32, (owned, 128), 1)
    for i in range(6):
        other = tail[(6 + i % 2) * owned : (7 + i % 2) * owned]
        shift = rows - 32 * (i // 2)
        other = jnp.concatenate([other[:, 128 - shift :], other[:, : 128 - shift]], axis=1)
        tail_b[z, i] = jnp.where(lanes < rows, tail[i * owned : (i + 1) * owned], other).astype(BF16)
    for sem in range(first):
        weight_start(1, sem)

    own_a = grad_a[pl.ds(pl.multiple_of(z * owned, 8), owned)]
    own_b = grad_b[pl.ds(pl.multiple_of(y * owned, 8), owned)]
    grad = jnp.concatenate([own_a[:, :rows], own_b[:, :rows]], axis=1)
    new_master, new_first, new_second = update(grad, states[0], states[1], states[2])
    new_master_ref[...] = new_master
    new_first_ref[...] = new_first
    new_second_ref[...] = new_second

    for pair in (relay[:2], relay[2:]):
        for lane in (0, 1):
            for sem, onward in pair:
                weight_landed(lane, sem)
                for k in onward:
                    weight_start(lane, k)
    weight_rest(1)
    for i in range(6):
        block = tail_b[:, i].reshape(width, 128).T
        out_ref[rows:, i * width : (i + 1) * width] = block[:rows]
        first_row = rows + 32 * (i // 2)
        first_col = (6 + i % 2) * width
        out_ref[first_row : first_row + 32, first_col : first_col + width] = block[rows:]
    weight_rest(0)
    remote(weight_came.at[0, 0], "z", 1, tally, tally).wait_send()


def finish_kernel(*refs):
    sources, targets, sems = refs[:6], refs[6:12], refs[12]
    copies = [pltpu.make_async_copy(s, t, sems.at[i]) for i, (s, t) in enumerate(zip(sources, targets))]
    for c in copies:
        c.start()
    for c in copies:
        c.wait()


def per_device(gradients, error_buffers, initial_q, master, first_moment, second_moment):
    rows, cols = gradients.shape[2:]
    rank = initial_q.shape[2]
    owned = master.shape[2]
    half = rank // 2
    width = cols // RING
    blocks = 2 * (RING - 1)
    exchanged = 3 * half * width + 2 * 24 * 128 + 4 * 128 + 3 * owned * 128 + rows // 2 * width // 2
    tally_rows = blocks * exchanged // 128
    vmem = pl.BlockSpec(memory_space=pltpu.VMEM)
    hbm = pl.BlockSpec(memory_space=pltpu.HBM)
    shapes = (
        jax.ShapeDtypeStruct((rows, cols), BF16),
        jax.ShapeDtypeStruct((rank, rows), F32),
        jax.ShapeDtypeStruct((owned, rows), F32),
        jax.ShapeDtypeStruct((owned, rows), F32),
        jax.ShapeDtypeStruct((owned, rows), F32),
        jax.ShapeDtypeStruct((rows, cols), BF16),
    )
    operands = (gradients[0, 0], error_buffers[0, 0], initial_q[0].T)
    operands += (master[0].T, first_moment[0].T, second_moment[0].T)
    outs = pl.pallas_call(
        step_kernel,
        name="relay_step",
        out_shape=tuple(pltpu.VMEM(x.shape, x.dtype) for x in shapes),
        in_specs=[hbm] * 6,
        out_specs=(vmem,) * 6,
        scratch_shapes=[
            pltpu.VMEM((rows, cols), BF16),
            pltpu.VMEM((rows, cols), BF16),
            pltpu.VMEM((rank, rows), F32),
            pltpu.VMEM((3, owned, rows), F32),
            pltpu.VMEM((RING, rank, width), F32),
            pltpu.VMEM((2, RING - 1, half, width), F32),
            pltpu.VMEM((2, RING, half, width), F32),
            pltpu.VMEM((RING, rank, width), F32),
            pltpu.VMEM((2, RING, 24, 128), F32),
            pltpu.VMEM((2, RING, 24, 128), F32),
            pltpu.VMEM((RING, 8, 128), F32),
            pltpu.VMEM((2, RING, 3, owned, 128), F32),
            pltpu.VMEM((width, 128), F32),
            pltpu.VMEM((width, 128), F32),
            pltpu.VMEM((RING, 6, owned, 128), BF16),
            pltpu.VMEM((tally_rows, 128), F32),
            pltpu.SemaphoreType.DMA((4,)),
            pltpu.SemaphoreType.DMA((1,)),
            pltpu.SemaphoreType.DMA((6, CHUNKS)),
            pltpu.SemaphoreType.DMA((4,)),
            pltpu.SemaphoreType.DMA((2, 2 * PIECES + 1)),
        ],
        compiler_params=pltpu.CompilerParams(
            collective_id=0, has_side_effects=True, vmem_limit_bytes=40 << 20
        ),
    )(*(pltpu.with_memory_space_constraint(x, pltpu.HBM) for x in operands))
    outs = pl.pallas_call(
        finish_kernel,
        name="finish",
        out_shape=shapes,
        in_specs=[vmem] * 6,
        out_specs=(hbm,) * 6,
        scratch_shapes=[pltpu.SemaphoreType.DMA((6,))],
    )(*(pltpu.with_memory_space_constraint(x, pltpu.VMEM) for x in outs))
    new_errors, right, new_master, new_first, new_second, gathered = outs
    return (
        new_errors[None, None],
        right.T[None],
        new_master.T[None],
        new_first.T[None],
        new_second.T[None],
        gathered[None],
    )


def solution(mesh):
    placed = (
        P("section", "dp", None, None),
        P("section", "dp", None, None),
        P("section", None, None),
        P("section", None, "dp"),
        P("section", None, "dp"),
        P("section", None, "dp"),
    )
    return jax.shard_map(
        per_device,
        mesh=mesh,
        in_specs=placed,
        out_specs=(
            P("section", "dp", None, None),
            P("section", None, None),
            P("section", None, "dp"),
            P("section", None, "dp"),
            P("section", None, "dp"),
            P("section", None, None),
        ),
        check_vma=False,
    )
```

```python
import functools

import jax
import jax.numpy as jnp
from jax import lax
from jax.experimental import pallas as pl
from jax.experimental.pallas import tpu as pltpu
from jax.sharding import PartitionSpec as P

STEP = 10


beta_one = 0.9
beta_two = 0.999
adam_epsilon = 1e-08
learn_rate = 0.02
clip_limit = 16.0

RING = 8
ROW_CHUNKS = 2
LANE_CHUNKS = 1
CHUNKS = ROW_CHUNKS * LANE_CHUNKS
PIECES = 2
ORDER = (4, 3, 5, 2, 6, 1, 7)
MESH = pl.DeviceIdType.MESH
HIGH = lax.Precision.HIGHEST
F32 = jnp.float32
BF16 = jnp.bfloat16


def dot_nn(a, b):
    return lax.dot_general(a, b, (((1,), (0,)), ((), ())), precision=HIGH, preferred_element_type=F32)


def dot_tn(a, b):
    return lax.dot_general(a, b, (((0,), (0,)), ((), ())), precision=HIGH, preferred_element_type=F32)


def dot_nt(a, b):
    return lax.dot_general(a, b, (((1,), (1,)), ((), ())), precision=HIGH, preferred_element_type=F32)


def three_parts(value):
    high = value.astype(BF16)
    rest = value - high.astype(F32)
    middle = rest.astype(BF16)
    low = (rest - middle.astype(F32)).astype(BF16)
    return high, middle, low


def widen(gram):
    rank = gram.shape[0]
    rows = lax.broadcasted_iota(jnp.int32, (rank, 128), 0)
    lanes = lax.broadcasted_iota(jnp.int32, (rank, 128), 1)
    identity = jnp.where(lanes == rows + rank, 1.0, 0.0).astype(F32)
    wide = jnp.concatenate([gram, jnp.zeros((rank, 128 - rank), F32)], axis=1) + identity
    return wide, jnp.ones((rank, 128), F32)


def eliminate(state, first, last):
    wide, pivots = state
    rank = wide.shape[0]
    rows = lax.broadcasted_iota(jnp.int32, (rank, 128), 0)
    for k in range(first, last):
        column = jnp.broadcast_to(wide[:, k : k + 1], (rank, 128))
        pivot = jnp.broadcast_to(column[k : k + 1, :], (rank, 128))
        row = jnp.broadcast_to(wide[k : k + 1, :], (rank, 128))
        pivots = jnp.where(rows == k, pivot, pivots)
        factor = jnp.where(rows > k, column / pivot, 0.0)
        wide = wide - factor * row
    return wide, pivots


def step_kernel(
    g_hbm, e_hbm, q_hbm, master_hbm, first_hbm, second_hbm,
    err_ref, right_ref, new_master_ref, new_first_ref, new_second_ref, out_ref,
    g_ref, e_ref, q_ref, states, local, red, sums, full, folds, nexts,
    norms, pre, grad_a, grad_b, terms, tail_b, tally, loads, sent, landed, state_came, weight_came,
):
    section = lax.axis_index("section")
    dp = lax.axis_index("dp")
    y = lax.div(dp, RING)
    z = lax.rem(dp, RING)
    replicas = RING * RING
    rank = q_ref.shape[0]
    half = rank // 2
    width = g_ref.shape[1] // RING
    owned = master_hbm.shape[0]
    rows = g_ref.shape[0] // 2

    def up(i, d):
        return lax.rem(i + d, RING)

    def down(i, d):
        return lax.rem(i + RING - d, RING)

    def peer(axis, d):
        if axis == "z":
            return (section, y * RING + up(z, d))
        if axis == "y":
            return (section, up(y, d) * RING + z)
        return (up(section, d), dp)

    def remote(recv_sem, axis, d, src, dst):
        return pltpu.make_async_remote_copy(
            src_ref=src, dst_ref=dst, send_sem=sent.at[0], recv_sem=recv_sem,
            device_id=peer(axis, d), device_id_type=MESH,
        )

    def send(phase, axis, d, src, dst, chunk=0):
        remote(landed.at[phase, chunk], axis, d, src, dst).start()

    def gathered(phase, view, chunk=0):
        remote(landed.at[phase, chunk], "z", 1, view, view).wait_recv()

    middle = (RING // 2) * width
    fetch = [(0, q_hbm, q_ref)]
    for i in range(2):
        cols = pl.ds(i * middle, middle)
        fetch += [(1 + i, g_hbm.at[:, cols], g_ref.at[:, cols]), (1 + i, e_hbm.at[:, cols], e_ref.at[:, cols])]
    fetch += [(3, x, states.at[i]) for i, x in enumerate((first_hbm, second_hbm, master_hbm))]
    for i, x, v in fetch:
        pltpu.make_async_copy(x, v, loads.at[i]).start()

    def loaded(i, view):
        pltpu.make_async_copy(view, view, loads.at[i]).wait()

    barrier = pltpu.get_barrier_semaphore()
    for axis in ("z", "y", "s"):
        for d in range(1, RING):
            pl.semaphore_signal(barrier, 1, device_id=peer(axis, d), device_id_type=MESH)

    loaded(0, q_ref)
    parts = jnp.concatenate(three_parts(q_ref[...]), axis=0)
    for j in range(RING):
        if j % (RING // 2) == 0:
            loaded(1 + j // (RING // 2), g_ref)
        cols = pl.ds(j * width, width)
        term = jnp.dot(parts, g_ref[:, cols], preferred_element_type=F32)
        term += jnp.dot(parts, e_ref[:, cols], preferred_element_type=F32)
        local[j] = term[:rank] + term[rank : 2 * rank] + term[2 * rank :]
    pl.semaphore_wait(barrier, 3 * (RING - 1))

    def state_step(step):
        if step > 1:
            view = pre.at[0, pl.ds(0, 4 if step <= RING // 2 else 2)]
            remote(state_came.at[step - 2], "z", 1, view, view).wait_recv()
        if step > RING // 2:
            return
        for lane, (axis, place) in enumerate((("z", z), ("y", y))):
            for way, block in enumerate((down(place, step - 1), up(place, step - 1))):
                view = pre.at[lane, block]
                if step == RING // 2:
                    view = pre.at[lane, block, :, pl.ds(owned // 2 * way, owned // 2)]
                remote(state_came.at[step - 1], axis, (1, RING - 1)[way], view, view).start()

    step = half // ROW_CHUNKS
    span = width // LANE_CHUNKS
    chunks = range(CHUNKS)

    def near(c):
        return pl.ds(c // LANE_CHUNKS * step, step), pl.ds(c % LANE_CHUNKS * span, span)

    def far(c):
        return pl.ds(half + c // LANE_CHUNKS * step, step), pl.ds(c % LANE_CHUNKS * span, span)

    for c in chunks:
        for d in ORDER:
            send(0, "z", d, local.at[up(z, d), *near(c)], red.at[0, d - 1, *near(c)], c)
            send(0, "y", d, local.at[up(y, d), *far(c)], red.at[1, d - 1, *near(c)], c)
    loaded(3, states)
    for i in range(3):
        value = states[i]
        pre[0, z, i] = value[:, :128]
        pre[1, y, i] = jnp.concatenate([value[:, rows:], value[:, : 128 - rows]], axis=1)
    state_step(1)
    others = pl.ds(0, RING - 1)
    for c in chunks:
        gathered(0, red.at[:, :, *near(c)], c)
        total_a = local[z, *near(c)]
        total_b = local[y, *far(c)]
        for i in range(RING - 1):
            total_a += red[0, i, *near(c)]
            total_b += red[1, i, *near(c)]
        sums[0, y, *near(c)] = total_a
        sums[1, z, *near(c)] = total_b
        for d in ORDER:
            send(1, "y", d, sums.at[0, y, *near(c)], sums.at[0, y, *near(c)], c)
            send(1, "z", d, sums.at[1, z, *near(c)], sums.at[1, z, *near(c)], c)
    state_step(2)
    for c in chunks:
        gathered(1, sums.at[:, others, *near(c)], c)
        total_a = sums[0, 0, *near(c)]
        total_b = sums[1, 0, *near(c)]
        for i in range(1, RING):
            total_a += sums[0, i, *near(c)]
            total_b += sums[1, i, *near(c)]
        full[z, *near(c)] = total_a
        full[y, *far(c)] = total_b
        for d in ORDER:
            send(2, "z", d, full.at[z, *near(c)], full.at[z, *near(c)], c)
            send(2, "y", d, full.at[y, *far(c)], full.at[y, *far(c)], c)
    state_step(3)
    for c in chunks:
        gathered(2, full.at[others, pl.ds(0, 2 * step), pl.ds(0, span)], c)

    whole = jnp.concatenate([full[j] for j in range(RING)], axis=1)
    parts = jnp.concatenate(three_parts(whole), axis=0)
    right = sum(
        lax.dot_general(parts, source[...], (((1,), (1,)), ((), ())), preferred_element_type=F32)
        for source in (g_ref, e_ref)
    )
    right = right[:rank] + right[rank : 2 * rank] + right[2 * rank :]
    rest = jnp.concatenate([right[:half, 128:192], right[half:, 128:192]], axis=1)
    folds[0, z, 0:16] = right[:half, :128]
    folds[0, z, 16:24] = rest[:8]
    folds[1, y, 0:16] = right[half:, :128]
    folds[1, y, 16:24] = rest[8:]
    for d in ORDER:
        send(3, "z", d, folds.at[0, z], folds.at[0, z])
        send(3, "y", d, folds.at[1, y], folds.at[1, y])
    state_step(4)

    gram = jnp.zeros((rank, rank), F32)
    for j in range(RING):
        gram += dot_nt(full[j], full[j])
    state = eliminate(widen(gram), 0, rank // 2)

    gathered(3, folds.at[:, others])
    total_a = folds[0, 0]
    total_b = folds[1, 0]
    for i in range(1, RING):
        total_a += folds[0, i]
        total_b += folds[1, i]
    nexts[0, y] = total_a
    nexts[1, z] = total_b
    for d in ORDER:
        send(4, "y", d, nexts.at[0, y], nexts.at[0, y])
        send(4, "z", d, nexts.at[1, z], nexts.at[1, z])

    wide, pivots = eliminate(state, rank // 2, rank)
    inverse = (wide * lax.rsqrt(pivots))[:, rank : 2 * rank]
    from_col = lax.broadcasted_iota(jnp.int32, (width, width), 0)
    to_col = lax.broadcasted_iota(jnp.int32, (width, width), 1)
    picked = jnp.zeros((3 * rank, width), F32)
    for i in range(RING):
        chosen = jnp.where(
            (from_col - owned * z == to_col - owned * i) & (to_col >= owned * i) & (to_col < owned * (i + 1)),
            1.0, 0.0,
        ).astype(BF16)
        parts = jnp.concatenate(three_parts(full[i]), axis=0)
        picked += jnp.dot(parts, chosen, preferred_element_type=F32)
    picked = picked[:rank] + picked[rank : 2 * rank] + picked[2 * rank :]

    gathered(4, nexts.at[:, others])
    total_a = nexts[0, 0]
    total_b = nexts[1, 0]
    for i in range(1, RING):
        total_a += nexts[0, i]
        total_b += nexts[1, i]
    rest = jnp.concatenate([total_a[16:24], total_b[16:24]], axis=0)
    top = jnp.concatenate([total_a[0:16], total_b[0:16]], axis=0)
    rest = jnp.concatenate([rest[:, :64], rest[:, 64:]], axis=0)
    right = jnp.concatenate([top, rest], axis=1)
    right = dot_nn(inverse, right) * (1.0 / replicas)
    squares = jnp.sum(right * right, keepdims=True)
    norms[section] = jnp.broadcast_to(squares, (8, 128))
    for d in ORDER:
        send(5, "s", d, norms.at[section], norms.at[section])
    right_ref[...] = right
    state_step(5)

    coef = dot_tn(inverse, right)
    grad_a[...] = dot_tn(full[y], coef[:, :128])
    grad_b[...] = dot_tn(picked, jnp.concatenate([coef[:, rows:], coef[:, : 128 - rows]], axis=1))
    rate = learn_rate / (1.0 - beta_one**STEP)
    gain = 1.0 / (1.0 - beta_two**STEP)
    for lane, grad in enumerate((grad_a, grad_b)):
        terms[lane, 0] = (rate * beta_one) * pre[lane, :, 0].reshape(width, 128)
        terms[lane, 1] = (gain * beta_two) * pre[lane, :, 1].reshape(width, 128)
        terms[lane, 2] = grad[...] * grad[...]
    high, low, _ = three_parts(coef)
    left = jnp.concatenate([high, high, low], axis=0)
    for j in range(RING):
        cols = pl.ds(j * width, width)
        high, low, _ = three_parts(full[j])
        approx = lax.dot_general(
            left, jnp.concatenate([high, low, high], axis=0), (((0,), (0,)), ((), ())),
            preferred_element_type=F32,
        )
        combined = g_ref[:, cols].astype(F32) + e_ref[:, cols].astype(F32)
        err_ref[:, cols] = (combined - approx).astype(BF16)

    gathered(5, norms.at[others])
    squares = norms[0]
    for i in range(1, RING):
        squares += norms[i]
    clip = jnp.minimum(1.0, clip_limit / jnp.sqrt(squares))[0:1, 0:1]

    def update(grad, first, second, master):
        scaled = clip * grad
        new_first = beta_one * first + (1.0 - beta_one) * scaled
        new_second = beta_two * second + (1.0 - beta_two) * scaled * scaled
        spread = jnp.sqrt(new_second * gain) + adam_epsilon
        return master - rate * new_first / spread, new_first, new_second

    def group_update(grad, lane):
        move = terms[lane, 0] + (rate * (1.0 - beta_one) * clip) * grad
        spread = jnp.sqrt(terms[lane, 1] + (gain * (1.0 - beta_two) * clip * clip) * terms[lane, 2]) + adam_epsilon
        return pre[lane, :, 2].reshape(width, 128) - move / spread

    mine = pl.ds(pl.multiple_of(y * width, 128), width)
    out_ref[0:rows, mine] = group_update(grad_a[...], 0).astype(BF16).T[0:rows]

    if PIECES == 2:
        hops = (
            (2, 0, 0, 1), (-2, 0, 0, 1), (2, 0, 1, 1), (-2, 0, 1, 1),
            (1, 0, 0, 1), (-1, 0, 0, 1), (1, 0, 1, 1), (-1, 0, 1, 1),
            (2, -2, 0, 1), (1, -2, 0, 1), (1, -2, 1, 1), (-1, 2, 0, 1), (-1, 2, 1, 1), (-2, 2, 1, 1),
        )
        first, relay = 8, ((0, (8, 9)), (1, (11,)), (2, (10,)), (3, (13, 12)))
    else:
        hops = (
            (2, 0, 0, 2), (-2, 0, 0, 2), (1, 0, 0, 2), (-1, 0, 0, 2),
            (2, -2, 0, 1), (1, -2, 0, 2), (-2, 2, 1, 1), (-1, 2, 0, 2),
        )
        first, relay = 4, ((0, (4, 5)), (1, (6, 7)))

    def weight_copy(lane, sem, offset):
        axis, place = (("y", y), ("z", z))[lane]
        target, _, part, parts = hops[sem]
        block = up(place, offset % RING)
        if lane == 0:
            lanes = pl.ds(pl.multiple_of(block * width, 128), width)
            view = out_ref.at[pl.ds(part * (rows // 2), parts * (rows // 2)), lanes]
        else:
            view = tail_b.at[block, pl.ds(3 * part, 3 * parts)]
        came = weight_came.at[lane, min(sem, len(relay))]
        return remote(came, axis, target % RING, view, view)

    def weight_view(lane, blocks):
        return out_ref.at[pl.ds(0, rows), pl.ds(0, blocks * width)] if lane == 0 else tail_b.at[pl.ds(0, blocks)]

    def weight_rest(lane):
        view = weight_view(lane, RING - 3)
        remote(weight_came.at[lane, len(relay)], "z", 1, view, view).wait_recv()

    def weight_start(lane, sem):
        weight_copy(lane, sem, hops[sem][1]).start()

    def weight_landed(lane, sem):
        weight_copy(lane, sem, hops[sem][1] - hops[sem][0]).wait_recv()

    for sem in range(first):
        weight_start(0, sem)
    tail = group_update(grad_b[...], 1)
    lanes = lax.broadcasted_iota(jnp.int32, (owned, 128), 1)
    for i in range(6):
        other = tail[(6 + i % 2) * owned : (7 + i % 2) * owned]
        shift = rows - 32 * (i // 2)
        other = jnp.concatenate([other[:, 128 - shift :], other[:, : 128 - shift]], axis=1)
        tail_b[z, i] = jnp.where(lanes < rows, tail[i * owned : (i + 1) * owned], other).astype(BF16)
    for sem in range(first):
        weight_start(1, sem)

    own_a = grad_a[pl.ds(pl.multiple_of(z * owned, 8), owned)]
    own_b = grad_b[pl.ds(pl.multiple_of(y * owned, 8), owned)]
    grad = jnp.concatenate([own_a[:, :rows], own_b[:, :rows]], axis=1)
    new_master, new_first, new_second = update(grad, states[0], states[1], states[2])
    new_master_ref[...] = new_master
    new_first_ref[...] = new_first
    new_second_ref[...] = new_second

    for pair in (relay[:2], relay[2:]):
        for lane in (0, 1):
            for sem, onward in pair:
                weight_landed(lane, sem)
                for k in onward:
                    weight_start(lane, k)
    weight_rest(1)
    for i in range(6):
        block = tail_b[:, i].reshape(width, 128).T
        out_ref[rows:, i * width : (i + 1) * width] = block[:rows]
        first_row = rows + 32 * (i // 2)
        first_col = (6 + i % 2) * width
        out_ref[first_row : first_row + 32, first_col : first_col + width] = block[rows:]
    weight_rest(0)
    remote(weight_came.at[0, 0], "z", 1, tally, tally).wait_send()


def finish_kernel(*refs):
    sources, targets, sems = refs[:6], refs[6:12], refs[12]
    copies = [pltpu.make_async_copy(s, t, sems.at[i]) for i, (s, t) in enumerate(zip(sources, targets))]
    for c in copies:
        c.start()
    for c in copies:
        c.wait()


def per_device(gradients, error_buffers, initial_q, master, first_moment, second_moment):
    rows, cols = gradients.shape[2:]
    rank = initial_q.shape[2]
    owned = master.shape[2]
    half = rank // 2
    width = cols // RING
    blocks = 2 * (RING - 1)
    exchanged = 3 * half * width + 2 * 24 * 128 + 4 * 128 + 3 * owned * 128 + rows // 2 * width // 2
    tally_rows = blocks * exchanged // 128
    vmem = pl.BlockSpec(memory_space=pltpu.VMEM)
    hbm = pl.BlockSpec(memory_space=pltpu.HBM)
    shapes = (
        jax.ShapeDtypeStruct((rows, cols), BF16),
        jax.ShapeDtypeStruct((rank, rows), F32),
        jax.ShapeDtypeStruct((owned, rows), F32),
        jax.ShapeDtypeStruct((owned, rows), F32),
        jax.ShapeDtypeStruct((owned, rows), F32),
        jax.ShapeDtypeStruct((rows, cols), BF16),
    )
    operands = (gradients[0, 0], error_buffers[0, 0], initial_q[0].T)
    operands += (master[0].T, first_moment[0].T, second_moment[0].T)
    outs = pl.pallas_call(
        step_kernel,
        name="relay_step",
        out_shape=tuple(pltpu.VMEM(x.shape, x.dtype) for x in shapes),
        in_specs=[hbm] * 6,
        out_specs=(vmem,) * 6,
        scratch_shapes=[
            pltpu.VMEM((rows, cols), BF16),
            pltpu.VMEM((rows, cols), BF16),
            pltpu.VMEM((rank, rows), F32),
            pltpu.VMEM((3, owned, rows), F32),
            pltpu.VMEM((RING, rank, width), F32),
            pltpu.VMEM((2, RING - 1, half, width), F32),
            pltpu.VMEM((2, RING, half, width), F32),
            pltpu.VMEM((RING, rank, width), F32),
            pltpu.VMEM((2, RING, 24, 128), F32),
            pltpu.VMEM((2, RING, 24, 128), F32),
            pltpu.VMEM((RING, 8, 128), F32),
            pltpu.VMEM((2, RING, 3, owned, 128), F32),
            pltpu.VMEM((width, 128), F32),
            pltpu.VMEM((width, 128), F32),
            pltpu.VMEM((2, 3, width, 128), F32),
            pltpu.VMEM((RING, 6, owned, 128), BF16),
            pltpu.VMEM((tally_rows, 128), F32),
            pltpu.SemaphoreType.DMA((4,)),
            pltpu.SemaphoreType.DMA((1,)),
            pltpu.SemaphoreType.DMA((6, CHUNKS)),
            pltpu.SemaphoreType.DMA((4,)),
            pltpu.SemaphoreType.DMA((2, 2 * PIECES + 1)),
        ],
        compiler_params=pltpu.CompilerParams(
            collective_id=0, has_side_effects=True, vmem_limit_bytes=40 << 20
        ),
    )(*(pltpu.with_memory_space_constraint(x, pltpu.HBM) for x in operands))
    outs = pl.pallas_call(
        finish_kernel,
        name="finish",
        out_shape=shapes,
        in_specs=[vmem] * 6,
        out_specs=(hbm,) * 6,
        scratch_shapes=[pltpu.SemaphoreType.DMA((6,))],
    )(*(pltpu.with_memory_space_constraint(x, pltpu.VMEM) for x in outs))
    new_errors, right, new_master, new_first, new_second, gathered = outs
    return (
        new_errors[None, None],
        right.T[None],
        new_master.T[None],
        new_first.T[None],
        new_second.T[None],
        gathered[None],
    )


def solution(mesh):
    placed = (
        P("section", "dp", None, None),
        P("section", "dp", None, None),
        P("section", None, None),
        P("section", None, "dp"),
        P("section", None, "dp"),
        P("section", None, "dp"),
    )
    return jax.shard_map(
        per_device,
        mesh=mesh,
        in_specs=placed,
        out_specs=(
            P("section", "dp", None, None),
            P("section", None, None),
            P("section", None, "dp"),
            P("section", None, "dp"),
            P("section", None, "dp"),
            P("section", None, None),
        ),
        check_vma=False,
    )
```
